32 devices in a mesh: dp: 4 (over y, core), expert: 8 (over z, x).
Axes of the slice: x: 2, y: 2, z: 4, core: 2. Of those that a mesh axis runs over, the one named last changes fastest.
Arguments:
- feats: bfloat16 [4, 32, 128, 512], P('dp', 'expert'), may hold values from -6 to 6
- labels: int32 [4, 32, 128, 1], P('dp', 'expert'), may hold values from 0 to 7; in each aligned block of 512 rows (0 to 511, 512 to 1023, ..., all dimensions but the last counted through in order) at most 128 rows name the same one
- w_first: bfloat16 [8, 512, 2048], P('expert'), may hold values from -0.25 to 0.25
- w_second: bfloat16 [8, 2048, 256], P('expert'), may hold values from -0.125 to 0.125
- kernel: bfloat16 [27, 256, 256], replicated, may hold values from -0.078125 to 0.078125
- cotangent: bfloat16 [4, 32, 128, 256], P('dp', 'expert'), may hold values from -6 to 6
Outputs:
- imitated: bfloat16 [4, 32, 128, 256], P('dp', 'expert')
- feat_grad: bfloat16 [4, 32, 128, 512], P('dp', 'expert')
- grad_first: float32 [8, 512, 2048], P('expert', None, 'dp')
- grad_second: float32 [8, 2048, 256], P('expert', 'dp')
The draws below stay inside these ranges and needn't reach their ends.
Inputs may be any that keep to these rules, and one draw needn't show every extreme that they name: `labels`: within the 512 patches of one device (aligned blocks of 512 patches in grid order), no label occurs more than 128 times, and some label occurs exactly 128 times.
All inputs are finite; a program needn't handle non-finite values.
Results may differ from the reference program's by a relative error of at most 0.023.
Values may be sent and summed in bfloat16 or wider, within the bound.
A program may use at most 128 MiB of HBM per device.

```python
import math
import jax
import jax.numpy as jnp
import numpy as np
from jax import lax

D = 512
HID = 2048
C = 256
EXPERTS = 8
GZ = 128
TOK_DEV = 512
CAP = 128
NX = 4
NY = 32


def block_scale(stream_key, shape, shards, low, high):
    factor_of = 1.0
    for axis_at, blocks in shards:
        draws = jax.random.uniform(jax.random.fold_in(jax.random.fold_in(stream_key, 6), axis_at), (blocks,), jnp.float32, low / len(shards), high / len(shards))
        factor_of = factor_of * jnp.repeat(jnp.exp(draws), shape[axis_at] // blocks).reshape((-1,) + (1,) * (len(shape) - 1 - axis_at))
    return factor_of


def deal_out(stream_key, own, number, rows, amount, top, bound, lean):
    order = jax.random.permutation(stream_key, amount)
    crowded, ordinary = shares(amount, rows * top, bound, lean, True), shares(amount, rows * top, bound, lean, False)
    places = jnp.arange(amount)

    def named(sizes, offset_by):
        used = int((sizes > 0).sum())
        fixed = max(1, used // 4)
        moved = fixed + (places - fixed + offset_by * (used - fixed)) % max(1, amount - fixed)
        return jnp.zeros((amount,), jnp.int32).at[order[jnp.where(places < fixed, places, moved)]].set(jnp.asarray(sizes, jnp.int32))

    sizes = jnp.where(number % 4 == 0, named(crowded, number // 4), named(ordinary, number - number // 4 - 1))
    mixed = jax.random.permutation(jax.random.fold_in(own, 3), amount)
    source_of, sink = mixed[0:amount // 2 * 2:2], mixed[1:amount // 2 * 2:2]
    margin = jnp.minimum(sizes[source_of] - 1, bound - sizes[sink]) // 2
    margin = jnp.where((source_of == order[0]) | (sink == order[0]) | (sizes[sink] == 0), 0, jnp.maximum(margin, 0))
    moved = jax.random.randint(jax.random.fold_in(own, 4), (amount // 2,), 0, 1 << 20) % (margin + 1)
    sizes = sizes.at[source_of].add(-moved).at[sink].add(moved)
    items = jnp.searchsorted(jnp.cumsum(sizes), jnp.arange(rows * top), side="right").astype(jnp.int32)
    grid = items.reshape(top, rows).T
    grid = grid[jax.random.permutation(jax.random.fold_in(own, 1), rows)]
    offset_by = jax.random.randint(jax.random.fold_in(own, 2), (rows, 1), 0, top)
    return jnp.take_along_axis(grid, (jnp.arange(top)[None, :] + offset_by) % top, axis=1)


def shares(count, total, limit, slope, full):
    portions = [(1 << 20) // math.isqrt(standing ** slope) + 1 for standing in range(1, count + 1)]
    largest = limit if full else min(limit, max(-(-total // count), total * portions[0] // sum(portions)))
    least = 1 if total - largest >= count - 1 else 0
    counts, rest = [largest] + [least] * (count - 1), total - largest - least * (count - 1)
    while rest > 0:
        candidates = [i for i in range(1, count) if counts[i] < largest] or [i for i in range(1, count) if counts[i] < limit]
        pool, left = sum([portions[i] for i in candidates]), rest
        for i in candidates:
            extra = min(limit - counts[i], max(1, left * portions[i] // pool), rest)
            counts[i] = counts[i] + extra
            rest = rest - extra
    return np.array(counts)


def noise(own_key, shape, width, bound, cuts=(), held_as=jnp.bfloat16):
    drawn = jax.random.normal(own_key, shape, jnp.float32) * width
    if len(cuts) > 0:
        drawn = block_scale(own_key, shape, cuts, -0.22, 0.18) * drawn
    return jnp.clip(drawn, min=-bound, max=bound).astype(held_as)


def setup_inputs(seed: int = 0) -> dict:
    streams_of = jax.random.split(jax.random.key(seed), 7)
    feats = noise(streams_of[0], (NX, NY, GZ, D), 1.0, 6.0, ((0, 4), (1, 8)))
    labels_keys = jax.random.split(jax.random.fold_in(streams_of[1], 1), NX * NY * GZ // TOK_DEV)
    labels_turns = jax.random.permutation(jax.random.fold_in(streams_of[1], 3), NX * NY * GZ // TOK_DEV)
    labels = jax.vmap(lambda own, number: deal_out(jax.random.fold_in(streams_of[1], 2), own, number, TOK_DEV, EXPERTS, 1, CAP, 2))(labels_keys, labels_turns).reshape((NX, NY, GZ, 1))
    w_first = noise(streams_of[2], (EXPERTS, D, HID), D ** -0.5, 0.25, ((0, 8),))
    w_second = noise(streams_of[3], (EXPERTS, HID, C), HID ** -0.5, 0.125, ((0, 8),))
    kernel = noise(streams_of[4], (27, C, C), (27 * C) ** -0.5, 0.078125)
    cotangent = noise(streams_of[5], (NX, NY, GZ, C), 1.0, 6.0, ((0, 4), (1, 8)))
    return dict(feats=feats, labels=labels, w_first=w_first, w_second=w_second, kernel=kernel, cotangent=cotangent)


def gelu_act(value):
    return jax.nn.gelu(value, approximate=True)

def gelu_back(preact, upstream):
    return jax.vjp(gelu_act, preact)[1](upstream)[0]

def convolve(field, kernel):
    taps = kernel.astype(jnp.float32).reshape(3, 3, 3, C, C)
    result = lax.conv_general_dilated(field[None], taps, (1, 1, 1), 'SAME', dimension_numbers=('NDHWC', 'DHWIO', 'NDHWC'), precision=lax.Precision.HIGHEST)
    return result[0]

def reference(feats, labels, w_first, w_second, kernel, cotangent):
    patches = NX * NY * GZ
    blocks = patches // TOK_DEV
    flat_feats = feats.reshape(patches, D)
    regime = labels.reshape(patches).astype(jnp.int32)
    onehot = (regime.reshape(blocks, TOK_DEV)[:, :, None] == jnp.arange(EXPERTS, dtype=jnp.int32)[None, None, :]).astype(jnp.int32)
    ranking = jnp.cumsum(onehot, axis=1) - 1
    slot_index = lax.optimization_barrier(jnp.sum(ranking * onehot, axis=2)).reshape(patches)
    block_id = jnp.arange(patches, dtype=jnp.int32) // TOK_DEV
    position = (block_id * CAP + slot_index).astype(jnp.int32)
    table = jnp.full((EXPERTS, blocks * CAP), patches, jnp.int32).at[regime, position].set(jnp.arange(patches, dtype=jnp.int32))
    feats_ext = jnp.concatenate([flat_feats, jnp.zeros((1, D), jnp.bfloat16)], axis=0)

    def forward(operands):
        first, second, index = operands
        row_block = feats_ext[index]
        preact = jnp.dot(row_block, first, preferred_element_type=jnp.float32)
        activation = gelu_act(preact).astype(jnp.bfloat16)
        return jnp.dot(activation, second, preferred_element_type=jnp.float32).astype(jnp.bfloat16)
    out_buffer = lax.map(forward, (w_first, w_second, table))
    expert_out = out_buffer[regime, position].reshape(NX, NY, GZ, C)
    conv_out, conv_vjp = jax.vjp(lambda field: convolve(field, kernel), expert_out.astype(jnp.float32))
    imitated = conv_out.astype(jnp.bfloat16)
    field_grad = conv_vjp(cotangent.astype(jnp.float32))[0].astype(jnp.bfloat16).reshape(patches, C)
    grad_ext = jnp.concatenate([field_grad, jnp.zeros((1, C), jnp.bfloat16)], axis=0)

    def backward(operands):
        first, second, index = operands
        row_block = feats_ext[index]
        preact = jnp.dot(row_block, first, preferred_element_type=jnp.float32)
        activation = gelu_act(preact).astype(jnp.bfloat16)
        grad_rows = grad_ext[index]
        upstream = jnp.dot(grad_rows, second.T, preferred_element_type=jnp.float32)
        gate_grad = gelu_back(preact, upstream).astype(jnp.bfloat16)
        input_grad = jnp.dot(gate_grad, first.T, preferred_element_type=jnp.float32).astype(jnp.bfloat16)
        grad_one = jnp.dot(row_block.T, gate_grad, preferred_element_type=jnp.float32)
        grad_two = jnp.dot(activation.T, grad_rows, preferred_element_type=jnp.float32)
        return (input_grad, grad_one, grad_two)
    input_buffer, grad_first, grad_second = lax.map(backward, (w_first, w_second, table))
    feat_grad = input_buffer[regime, position].reshape(NX, NY, GZ, D)
    return (imitated, feat_grad, grad_first, grad_second)
```

```python
import functools

import jax
import jax.numpy as jnp
from jax import lax
from jax.experimental import pallas as pl
from jax.experimental.pallas import tpu as pltpu
from jax.sharding import PartitionSpec as P

BF16 = jnp.bfloat16
F32 = jnp.float32
ROOT = 0.7978845608028654
CUBIC = 0.044715


def dot(a, b):
    return jnp.dot(a, b, preferred_element_type=F32)


def dot_t(a, b):
    return lax.dot_general(a, b, (((1,), (1,)), ((), ())), preferred_element_type=F32)


def remote(src, dst, send, recv, **device):
    return pltpu.make_async_remote_copy(
        src_ref=src,
        dst_ref=dst,
        send_sem=send,
        recv_sem=recv,
        device_id=device,
        device_id_type=pl.DeviceIdType.MESH,
    )


def shifted(value, step, depth):
    rows = value.shape[0]
    place = lax.broadcasted_iota(jnp.int32, value.shape, 0) % depth
    if step > 0:
        return jnp.where(place == 0, 0.0, pltpu.roll(value, 1, 0))
    return jnp.where(place == depth - 1, 0.0, pltpu.roll(value, rows - 1, 0))


def convolved(grid, taps, rows, depth, flipped):
    channels = taps.shape[1]
    tokens = rows * depth
    pieces, sums = [], []
    for a in range(3):
        for b in range(3):
            at, bt = (2 - a, 2 - b) if flipped else (a, b)
            pieces.append(grid[bt : bt + rows, at].reshape(tokens, channels))
    columns = jnp.concatenate(pieces, axis=1)
    for c in range(3):
        if flipped:
            weights = jnp.concatenate([taps[3 * k + c] for k in range(9)], axis=1)
            sums.append(dot_t(columns, weights))
        else:
            weights = jnp.concatenate([taps[3 * k + c] for k in range(9)], axis=0)
            sums.append(dot(columns, weights))
    first, last = (sums[2], sums[0]) if flipped else (sums[0], sums[2])
    return sums[1] + shifted(first, 1, depth) + shifted(last, -1, depth)


def kernel(
    n_dp, n_ex,
    labels, feats, cot, w1_hbm, w2_hbm, taps_hbm,
    imitated, feat_grad, grad_one, grad_two,
    w1, w2, taps, spread,
    out_f, in_f, out_g, in_g, out_o, in_o, out_b, in_b,
    act, slope, gate, grid_g, grid_o,
    part1, part2, pair1, pair2, sum1, sum2, far1, far2,
    load_sem, halo_send, halo_recv,
    f_send, f_recv, g_send, g_recv, o_send, o_recv, b_send, b_recv,
    pair_send, pair_recv, far_send, far_recv,
):
    tokens, width = feats.shape
    rows, depth, channels = cot.shape
    hidden = w1.shape[1]
    cap = in_f.shape[1]
    slots = n_ex * cap
    block = hidden // n_dp
    half = n_dp // 2
    dp = lax.axis_index("dp")
    me = lax.axis_index("expert")
    side = dp % 2
    level = dp // 2
    mate = dp + 1 - 2 * side

    loads = [
        pltpu.make_async_copy(w1_hbm, w1, load_sem.at[0]),
        pltpu.make_async_copy(w2_hbm, w2, load_sem.at[1]),
        pltpu.make_async_copy(taps_hbm, taps, load_sem.at[2]),
    ]
    loads[2].start()
    loads[0].start()
    loads[1].start()

    barrier = pltpu.get_barrier_semaphore()

    def greet_expert(d, carry):
        pl.semaphore_signal(
            barrier, inc=1, device_id={"expert": (me + d) % n_ex},
            device_id_type=pl.DeviceIdType.MESH,
        )
        return carry

    def greet_dp(d, carry):
        pl.semaphore_signal(
            barrier, inc=1, device_id={"dp": (dp + d) % n_dp},
            device_id_type=pl.DeviceIdType.MESH,
        )
        return carry

    lax.fori_loop(1, n_ex, greet_expert, 0)
    lax.fori_loop(1, n_dp, greet_dp, 0)

    relative = labels[...] - me
    relative = jnp.where(relative < 0, relative + n_ex, relative)
    named = lax.broadcasted_iota(jnp.int32, (n_ex, tokens), 0)
    hot = relative == named
    before = (
        lax.broadcasted_iota(jnp.int32, (tokens, tokens), 0)
        < lax.broadcasted_iota(jnp.int32, (tokens, tokens), 1)
    )
    rank = dot(jnp.where(hot, 1.0, 0.0).astype(BF16), jnp.where(before, 1.0, 0.0).astype(BF16))
    place = rank + (named * cap).astype(F32)
    target = jnp.sum(jnp.where(hot, place, 0.0), axis=0, keepdims=True)
    which = lax.broadcasted_iota(jnp.int32, (slots, tokens), 0).astype(F32)
    spread[...] = jnp.where(which == target, 1.0, 0.0).astype(BF16).reshape(n_ex, cap, tokens)

    grid_g[1 : rows + 1, 1] = cot[...]
    pl.semaphore_wait(barrier, n_ex + n_dp - 2)

    def halo(grid, at):
        inner = pl.ds(1, rows)
        return (
            (dp < n_dp - 1, dp > 0, remote(
                grid.at[inner, 1], grid.at[inner, 0],
                halo_send.at[at], halo_recv.at[at], dp=(dp + 1) % n_dp)),
            (dp > 0, dp < n_dp - 1, remote(
                grid.at[inner, 1], grid.at[inner, 2],
                halo_send.at[at + 1], halo_recv.at[at + 1], dp=(dp + n_dp - 1) % n_dp)),
            (me < n_ex - 1, me > 0, remote(
                grid.at[rows], grid.at[0],
                halo_send.at[at + 2], halo_recv.at[at + 2], expert=(me + 1) % n_ex)),
            (me > 0, me < n_ex - 1, remote(
                grid.at[1], grid.at[rows + 1],
                halo_send.at[at + 3], halo_recv.at[at + 3], expert=(me + n_ex - 1) % n_ex)),
        )

    def begin(steps):
        for sends, _, copy in steps:
            pl.when(sends)(copy.start)

    def landed(steps):
        for _, gets, copy in steps:
            pl.when(gets)(copy.wait_recv)

    def finish(steps):
        for sends, _, copy in steps:
            pl.when(sends)(copy.wait_send)

    def edges(grid):
        empty = jnp.zeros((rows, depth, channels), BF16)
        strip = jnp.zeros((3, depth, channels), BF16)

        @pl.when(dp == 0)
        def _():
            grid[1 : rows + 1, 0] = empty

        @pl.when(dp == n_dp - 1)
        def _():
            grid[1 : rows + 1, 2] = empty

        @pl.when(me == 0)
        def _():
            grid[0] = strip

        @pl.when(me == n_ex - 1)
        def _():
            grid[rows + 1] = strip

    halo_g, halo_o = halo(grid_g, 0), halo(grid_o, 4)
    begin(halo_g[:2])

    def turn(i):
        return n_ex // 2 + (1 - 2 * (i % 2)) * ((i + 1) // 2)

    def outward(src, dst, send, recv, d):
        return remote(src.at[d], dst.at[d], send.at[d], recv.at[d], expert=(me + d) % n_ex)

    def homeward(src, dst, send, recv, d):
        return remote(
            src.at[d], dst.at[d], send.at[d], recv.at[d], expert=(me + n_ex - d) % n_ex
        )

    def send_feats(i, carry):
        d = turn(i)
        out_f[d] = dot(spread[d], feats[...]).astype(BF16)
        outward(out_f, in_f, f_send, f_recv, d).start()
        return carry

    lax.fori_loop(0, 3, send_feats, 0)
    edges(grid_g)
    landed(halo_g[:2])
    begin(halo_g[2:])
    lax.fori_loop(3, n_ex - 1, send_feats, 0)
    in_f[0] = dot(spread[0], feats[...]).astype(BF16)

    tile = min(hidden, 512)

    def forward(d, result):
        row_block = in_f[d]
        for at in range(0, hidden, tile):
            v = dot(row_block, w1[:, at : at + tile])
            square = v * v
            t = jnp.tanh(v * (ROOT + (ROOT * CUBIC) * square))
            half_up = 0.5 + 0.5 * t
            act[d, :, at : at + tile] = (v * half_up).astype(BF16)
            inner = ROOT + (3.0 * ROOT * CUBIC) * square
            slope[d, :, at : at + tile] = half_up + (0.5 * v) * (1.0 - t * t) * inner
        result[d] = dot(act[d], w2[...]).astype(BF16)

    loads[0].wait()
    loads[1].wait()
    forward(0, in_o)
    landed(halo_g[2:])
    loads[2].wait()
    field_grad = convolved(grid_g, taps, rows, depth, True).astype(BF16)
    finish(halo_g)
    grid_o[1 : rows + 1, 1] = field_grad.reshape(rows, depth, channels)

    def send_grads(i, carry):
        d = turn(i)
        out_g[d] = dot(spread[d], grid_o[1 : rows + 1, 1].reshape(tokens, channels)).astype(BF16)
        outward(out_g, in_g, g_send, g_recv, d).start()
        return carry

    lax.fori_loop(0, n_ex - 1, send_grads, 0)
    in_g[0] = dot(spread[0], grid_o[1 : rows + 1, 1].reshape(tokens, channels)).astype(BF16)

    def go_forward(i, carry):
        d = turn(i)
        outward(out_f, in_f, f_send, f_recv, d).wait_recv()
        forward(d, out_o)
        homeward(out_o, in_o, o_send, o_recv, d).start()
        return carry

    lax.fori_loop(0, n_ex - 1, go_forward, 0)

    def backward(d, result):
        grads = in_g[d]
        for at in range(0, hidden, tile):
            up = dot_t(grads, w2[at : at + tile, :])
            gate[d, :, at : at + tile] = (up * slope[d, :, at : at + tile]).astype(BF16)
        result[d] = dot_t(gate[d], w1[...]).astype(BF16)

    def go_backward(i, carry):
        d = turn(i)
        outward(out_g, in_g, g_send, g_recv, d).wait_recv()
        backward(d, out_b)
        homeward(out_b, in_b, b_send, b_recv, d).start()
        return carry

    backward(0, in_b)
    lax.fori_loop(0, n_ex - 1, go_backward, 0)

    feats_t = in_f[...].reshape(slots, width).T
    grads_t = in_g[...].reshape(slots, channels).T
    for owner in range(n_dp):
        cols = slice(owner * block, (owner + 1) * block)
        part1[owner % 2, owner // 2] = dot(
            feats_t, gate[:, :, cols].reshape(slots, block)).astype(BF16)
        part2[owner % 2, owner // 2] = dot(
            grads_t, act[:, :, cols].reshape(slots, block)).astype(BF16)
    pair = (
        remote(part1.at[1 - side], pair1, pair_send.at[0], pair_recv.at[0], dp=mate),
        remote(part2.at[1 - side], pair2, pair_send.at[1], pair_recv.at[1], dp=mate),
    )
    for copy in pair:
        copy.start()

    def got_outs(i, carry):
        homeward(out_o, in_o, o_send, o_recv, turn(i)).wait_recv()
        return carry

    lax.fori_loop(0, n_ex - 1, got_outs, 0)
    back = spread[...].reshape(slots, tokens).T
    mixed = dot(back, in_o[...].reshape(slots, channels)).astype(BF16)
    grid_o[1 : rows + 1, 1] = mixed.reshape(rows, depth, channels)
    begin(halo_o[:2])
    edges(grid_o)

    for copy in pair:
        copy.wait()
    far = []
    for o in range(1, half):
        other = (level + o) % half
        sum1[o] = (part1[side, other].astype(F32) + pair1[other].astype(F32)).astype(BF16)
        sum2[o] = (part2[side, other].astype(F32) + pair2[other].astype(F32)).astype(BF16)
        to = 2 * other + side
        far.append(remote(
            sum1.at[o], far1.at[o], far_send.at[0, o], far_recv.at[0, o], dp=to))
        far.append(remote(
            sum2.at[o], far2.at[o], far_send.at[1, o], far_recv.at[1, o], dp=to))
    landed(halo_o[:2])
    begin(halo_o[2:])
    for copy in far:
        copy.start()
    landed(halo_o[2:])
    imitated[...] = convolved(grid_o, taps, rows, depth, False).astype(BF16)
    finish(halo_o)
    for copy in far:
        copy.wait()
    total1 = part1[side, level].astype(F32) + pair1[level].astype(F32)
    total2 = part2[side, level].astype(F32) + pair2[level].astype(F32)
    for o in range(1, half):
        total1 = total1 + far1[o].astype(F32)
        total2 = total2 + far2[o].astype(F32)
    grad_one[...] = total1
    grad_two[...] = total2.T

    def got_back(i, carry):
        homeward(out_b, in_b, b_send, b_recv, turn(i)).wait_recv()
        return carry

    lax.fori_loop(0, n_ex - 1, got_back, 0)
    feat_grad[...] = dot(back, in_b[...].reshape(slots, width)).astype(BF16)

    def drained(i, carry):
        d = turn(i)
        outward(out_f, in_f, f_send, f_recv, d).wait_send()
        outward(out_g, in_g, g_send, g_recv, d).wait_send()
        homeward(out_o, in_o, o_send, o_recv, d).wait_send()
        homeward(out_b, in_b, b_send, b_recv, d).wait_send()
        return carry

    lax.fori_loop(0, n_ex - 1, drained, 0)


def per_device(feats, labels, w_first, w_second, taps, cotangent):
    n_dp = lax.axis_size("dp")
    n_ex = lax.axis_size("expert")
    rows, depth, width = feats.shape[1:]
    channels = taps.shape[2]
    hidden = w_first.shape[2]
    tokens = rows * depth
    cap = 2 * tokens // n_ex
    block = hidden // n_dp
    half = n_dp // 2
    vmem = pl.BlockSpec(memory_space=pltpu.VMEM)
    hbm = pl.BlockSpec(memory_space=pl.ANY)
    wide = pltpu.VMEM((n_ex, cap, width), BF16)
    thin = pltpu.VMEM((n_ex, cap, channels), BF16)
    grid = pltpu.VMEM((rows + 2, 3, depth, channels), BF16)
    dma = pltpu.SemaphoreType.DMA
    outs = pl.pallas_call(
        functools.partial(kernel, n_dp, n_ex),
        out_shape=(
            jax.ShapeDtypeStruct((tokens, channels), BF16),
            jax.ShapeDtypeStruct((tokens, width), BF16),
            jax.ShapeDtypeStruct((width, block), F32),
            jax.ShapeDtypeStruct((block, channels), F32),
        ),
        in_specs=[vmem, vmem, vmem, hbm, hbm, hbm],
        out_specs=(vmem,) * 4,
        scratch_shapes=[
            pltpu.VMEM((width, hidden), BF16),
            pltpu.VMEM((hidden, channels), BF16),
            pltpu.VMEM(taps.shape, BF16),
            pltpu.VMEM((n_ex, cap, tokens), BF16),
            wide, wide, thin, thin, thin, thin, wide, wide,
            pltpu.VMEM((n_ex, cap, hidden), BF16),
            pltpu.VMEM((n_ex, cap, hidden), F32),
            pltpu.VMEM((n_ex, cap, hidden), BF16),
            grid, grid,
            pltpu.VMEM((2, half, width, block), BF16),
            pltpu.VMEM((2, half, channels, block), BF16),
            pltpu.VMEM((half, width, block), BF16),
            pltpu.VMEM((half, channels, block), BF16),
            pltpu.VMEM((half, width, block), BF16),
            pltpu.VMEM((half, channels, block), BF16),
            pltpu.VMEM((half, width, block), BF16),
            pltpu.VMEM((half, channels, block), BF16),
            dma((3,)), dma((8,)), dma((8,)),
            dma((n_ex,)), dma((n_ex,)), dma((n_ex,)), dma((n_ex,)),
            dma((n_ex,)), dma((n_ex,)), dma((n_ex,)), dma((n_ex,)),
            dma((2,)), dma((2,)), dma((2, half)), dma((2, half)),
        ],
        compiler_params=pltpu.CompilerParams(
            collective_id=0, has_side_effects=True, vmem_limit_bytes=60 * 2**20
        ),
        name="routed_experts",
    )(
        labels.reshape(1, tokens),
        feats.reshape(tokens, width),
        cotangent.reshape(rows, depth, channels),
        w_first[0],
        w_second[0],
        taps,
    )
    imitated, feat_grad, grad_one, grad_two = outs
    return (
        imitated.reshape(1, rows, depth, channels),
        feat_grad.reshape(1, rows, depth, width),
        grad_one[None],
        grad_two[None],
    )


def solution(mesh):
    in_specs = (
        P("dp", "expert", None, None),
        P("dp", "expert", None, None),
        P("expert", None, None),
        P("expert", None, None),
        P(),
        P("dp", "expert", None, None),
    )
    out_specs = (
        P("dp", "expert", None, None),
        P("dp", "expert", None, None),
        P("expert", None, "dp"),
        P("expert", "dp", None),
    )
    return jax.shard_map(
        per_device, mesh=mesh, in_specs=in_specs, out_specs=out_specs, check_vma=False
    )
```

```python
import functools

import jax
import jax.numpy as jnp
from jax import lax
from jax.experimental import pallas as pl
from jax.experimental.pallas import tpu as pltpu
from jax.sharding import PartitionSpec as P

BF16 = jnp.bfloat16
F32 = jnp.float32
ROOT = 0.7978845608028654
CUBIC = 0.044715


def dot(a, b):
    return jnp.dot(a, b, preferred_element_type=F32)


def dot_t(a, b):
    return lax.dot_general(a, b, (((1,), (1,)), ((), ())), preferred_element_type=F32)


def remote(src, dst, send, recv, **device):
    return pltpu.make_async_remote_copy(
        src_ref=src,
        dst_ref=dst,
        send_sem=send,
        recv_sem=recv,
        device_id=device,
        device_id_type=pl.DeviceIdType.MESH,
    )


def shifted(value, step, depth):
    rows = value.shape[0]
    place = lax.broadcasted_iota(jnp.int32, value.shape, 0) % depth
    if step > 0:
        return jnp.where(place == 0, 0.0, pltpu.roll(value, 1, 0))
    return jnp.where(place == depth - 1, 0.0, pltpu.roll(value, rows - 1, 0))


def convolved(grid, taps, rows, depth, flipped):
    channels = taps.shape[1]
    tokens = rows * depth
    pieces, sums = [], []
    for a in range(3):
        for b in range(3):
            at, bt = (2 - a, 2 - b) if flipped else (a, b)
            pieces.append(grid[bt : bt + rows, at].reshape(tokens, channels))
    columns = jnp.concatenate(pieces, axis=1)
    for c in range(3):
        if flipped:
            weights = jnp.concatenate([taps[3 * k + c] for k in range(9)], axis=1)
            sums.append(dot_t(columns, weights))
        else:
            weights = jnp.concatenate([taps[3 * k + c] for k in range(9)], axis=0)
            sums.append(dot(columns, weights))
    first, last = (sums[2], sums[0]) if flipped else (sums[0], sums[2])
    return sums[1] + shifted(first, 1, depth) + shifted(last, -1, depth)


def kernel(
    n_dp, n_ex,
    labels, feats, cot, w1_hbm, w2_hbm, taps_hbm,
    imitated, feat_grad, grad_one, grad_two,
    w1, w2, taps, spread,
    out_f, in_f, out_g, in_g, out_o, in_o, out_b, in_b,
    act, slope, gate, grid_g, grid_o,
    part1, part2, pair1, pair2, sum1, sum2, far1, far2,
    load_sem, halo_send, halo_recv,
    f_send, f_recv, g_send, g_recv, o_send, o_recv, b_send, b_recv,
    pair_send, pair_recv, far_send, far_recv,
):
    tokens, width = feats.shape
    rows, depth, channels = cot.shape
    hidden = w1.shape[1]
    cap = in_f.shape[1]
    slots = n_ex * cap
    block = hidden // n_dp
    half = n_dp // 2
    dp = lax.axis_index("dp")
    me = lax.axis_index("expert")
    side = dp % 2
    level = dp // 2
    mate = dp + 1 - 2 * side

    loads = [
        pltpu.make_async_copy(w1_hbm, w1, load_sem.at[0]),
        pltpu.make_async_copy(w2_hbm, w2, load_sem.at[1]),
        pltpu.make_async_copy(taps_hbm, taps, load_sem.at[2]),
    ]
    loads[2].start()
    loads[0].start()
    loads[1].start()

    barrier = pltpu.get_barrier_semaphore()

    def greet_expert(d, carry):
        pl.semaphore_signal(
            barrier, inc=1, device_id={"expert": (me + d) % n_ex},
            device_id_type=pl.DeviceIdType.MESH,
        )
        return carry

    def greet_dp(d, carry):
        pl.semaphore_signal(
            barrier, inc=1, device_id={"dp": (dp + d) % n_dp},
            device_id_type=pl.DeviceIdType.MESH,
        )
        return carry

    lax.fori_loop(1, n_ex, greet_expert, 0)
    lax.fori_loop(1, n_dp, greet_dp, 0)
    grid_g[1 : rows + 1, 1] = cot[...]

    relative = labels[...] - me
    relative = jnp.where(relative < 0, relative + n_ex, relative)
    relative = jnp.where(
        relative >= n_ex // 2, 2 * relative - n_ex, n_ex - 1 - 2 * relative)
    named = lax.broadcasted_iota(jnp.int32, (n_ex, tokens), 0)
    hot = relative == named
    before = (
        lax.broadcasted_iota(jnp.int32, (tokens, tokens), 0)
        < lax.broadcasted_iota(jnp.int32, (tokens, tokens), 1)
    )
    rank = dot(jnp.where(hot, 1.0, 0.0).astype(BF16), jnp.where(before, 1.0, 0.0).astype(BF16))
    place = rank + (named * cap).astype(F32)
    target = jnp.sum(jnp.where(hot, place, 0.0), axis=0, keepdims=True)
    which = lax.broadcasted_iota(jnp.int32, (cap, tokens), 0)

    def halo(grid, at):
        return (
            (me < n_ex - 1, me > 0, remote(
                grid.at[rows, 1], grid.at[0, 1],
                halo_send.at[at], halo_recv.at[at], expert=(me + 1) % n_ex)),
            (me > 0, me < n_ex - 1, remote(
                grid.at[1, 1], grid.at[rows + 1, 1],
                halo_send.at[at + 1], halo_recv.at[at + 1], expert=(me + n_ex - 1) % n_ex)),
            (dp < n_dp - 1, dp > 0, remote(
                grid.at[:, 1], grid.at[:, 0],
                halo_send.at[at + 2], halo_recv.at[at + 2], dp=(dp + 1) % n_dp)),
            (dp > 0, dp < n_dp - 1, remote(
                grid.at[:, 1], grid.at[:, 2],
                halo_send.at[at + 3], halo_recv.at[at + 3], dp=(dp + n_dp - 1) % n_dp)),
        )

    def begin(steps):
        for sends, _, copy in steps:
            pl.when(sends)(copy.start)

    def landed(steps):
        for _, gets, copy in steps:
            pl.when(gets)(copy.wait_recv)

    def finish(steps):
        for sends, _, copy in steps:
            pl.when(sends)(copy.wait_send)

    def edges(grid):
        slab = jnp.zeros((rows + 2, depth, channels), BF16)
        strip = jnp.zeros((depth, channels), BF16)

        @pl.when(dp == 0)
        def _():
            grid[:, 0] = slab

        @pl.when(dp == n_dp - 1)
        def _():
            grid[:, 2] = slab

        @pl.when(me == 0)
        def _():
            grid[0, 1] = strip

        @pl.when(me == n_ex - 1)
        def _():
            grid[rows + 1, 1] = strip

    halo_g, halo_o = halo(grid_g, 0), halo(grid_o, 4)
    pl.semaphore_wait(barrier, n_ex + n_dp - 2)
    begin(halo_g[:2])

    def turn(i):
        return n_ex // 2 + (1 - 2 * (i % 2)) * ((i + 1) // 2)

    def outward(src, dst, send, recv, i):
        return remote(
            src.at[i], dst.at[i], send.at[i], recv.at[i], expert=(me + turn(i)) % n_ex
        )

    def homeward(src, dst, send, recv, i):
        return remote(
            src.at[i], dst.at[i], send.at[i], recv.at[i], expert=(me + n_ex - turn(i)) % n_ex
        )

    def chosen(i):
        hit = (which + i * cap).astype(F32) == target
        return jnp.where(hit, 1.0, 0.0).astype(BF16)

    def send_feats(i, carry):
        spread[i] = chosen(i)
        out_f[i] = dot(spread[i], feats[...]).astype(BF16)
        outward(out_f, in_f, f_send, f_recv, i).start()
        return carry

    own = n_ex - 1
    lax.fori_loop(0, 2, send_feats, 0)
    edges(grid_g)
    landed(halo_g[:2])
    begin(halo_g[2:])
    lax.fori_loop(2, own, send_feats, 0)
    spread[own] = chosen(own)
    in_f[own] = dot(spread[own], feats[...]).astype(BF16)

    tile = min(hidden, 512)
    loads[2].wait()
    landed(halo_g[2:])
    field_grad = convolved(grid_g, taps, rows, depth, True).astype(BF16)
    grid_o[1 : rows + 1, 1] = field_grad.reshape(rows, depth, channels)

    def send_grads(i, carry):
        out_g[i] = dot(spread[i], grid_o[1 : rows + 1, 1].reshape(tokens, channels)).astype(BF16)
        outward(out_g, in_g, g_send, g_recv, i).start()
        return carry

    lax.fori_loop(0, own, send_grads, 0)
    in_g[own] = dot(spread[own], grid_o[1 : rows + 1, 1].reshape(tokens, channels)).astype(BF16)
    finish(halo_g)
    loads[0].wait()
    loads[1].wait()

    def forward(k):
        both = pl.ds(2 * k, 2)
        row_block = in_f[both].reshape(2 * cap, width)
        for at in range(0, hidden, tile):
            v = dot(row_block, w1[:, at : at + tile])
            square = v * v
            t = jnp.tanh(v * (ROOT + (ROOT * CUBIC) * square))
            half_up = 0.5 + 0.5 * t
            act[both, :, at : at + tile] = (v * half_up).astype(BF16).reshape(2, cap, tile)
            inner = ROOT + (3.0 * ROOT * CUBIC) * square
            grown = half_up + (0.5 * v) * (1.0 - t * t) * inner
            slope[both, :, at : at + tile] = grown.reshape(2, cap, tile)
        result = dot(act[both].reshape(2 * cap, hidden), w2[...])
        out_o[both] = result.astype(BF16).reshape(2, cap, channels)

    def go_forward(k, carry):
        for i in (2 * k, 2 * k + 1):
            outward(out_f, in_f, f_send, f_recv, i).wait_recv()
        forward(k)
        for i in (2 * k, 2 * k + 1):
            homeward(out_o, in_o, o_send, o_recv, i).start()
        return carry

    pairs = n_ex // 2
    lax.fori_loop(0, pairs - 1, go_forward, 0)
    outward(out_f, in_f, f_send, f_recv, own - 1).wait_recv()
    forward(pairs - 1)
    homeward(out_o, in_o, o_send, o_recv, own - 1).start()
    in_o[own] = out_o[own]

    def backward(k):
        both = pl.ds(2 * k, 2)
        grads = in_g[both].reshape(2 * cap, channels)
        for at in range(0, hidden, tile):
            up = dot_t(grads, w2[at : at + tile, :])
            scale = slope[both, :, at : at + tile].reshape(2 * cap, tile)
            gate[both, :, at : at + tile] = (up * scale).astype(BF16).reshape(2, cap, tile)
        result = dot_t(gate[both].reshape(2 * cap, hidden), w1[...])
        out_b[both] = result.astype(BF16).reshape(2, cap, width)

    def go_backward(k, carry):
        for i in (2 * k, 2 * k + 1):
            outward(out_g, in_g, g_send, g_recv, i).wait_recv()
        backward(k)
        for i in (2 * k, 2 * k + 1):
            homeward(out_b, in_b, b_send, b_recv, i).start()
        return carry

    lax.fori_loop(0, pairs // 2, go_backward, 0)

    def got_outs(i, carry):
        homeward(out_o, in_o, o_send, o_recv, i).wait_recv()
        return carry

    lax.fori_loop(0, own, got_outs, 0)
    back = spread[...].reshape(slots, tokens).T
    mixed = dot(back, in_o[...].reshape(slots, channels)).astype(BF16)
    grid_o[1 : rows + 1, 1] = mixed.reshape(rows, depth, channels)
    begin(halo_o[:2])
    edges(grid_o)
    lax.fori_loop(pairs // 2, pairs - 1, go_backward, 0)
    outward(out_g, in_g, g_send, g_recv, own - 1).wait_recv()
    backward(pairs - 1)
    homeward(out_b, in_b, b_send, b_recv, own - 1).start()
    in_b[own] = out_b[own]
    landed(halo_o[:2])
    begin(halo_o[2:])

    feats_t = in_f[...].reshape(slots, width).T
    grads_t = in_g[...].reshape(slots, channels).T
    pair = {}
    for o in list(range(1, half)) + [0]:
        other = (level + o) % half
        for parity in range(2):
            start = pl.multiple_of((2 * other + parity) * block, block)
            part1[parity, other] = dot(
                feats_t, gate[:, :, pl.ds(start, block)].reshape(slots, block)).astype(BF16)
            part2[parity, other] = dot(
                grads_t, act[:, :, pl.ds(start, block)].reshape(slots, block)).astype(BF16)
        pair[o] = (
            remote(part1.at[1 - side, other], pair1.at[o],
                   pair_send.at[0, o], pair_recv.at[0, o], dp=mate),
            remote(part2.at[1 - side, other], pair2.at[o],
                   pair_send.at[1, o], pair_recv.at[1, o], dp=mate),
        )
        for copy in pair[o]:
            copy.start()
    far = []
    for o in range(1, half):
        other = (level + o) % half
        for copy in pair[o]:
            copy.wait()
        sum1[o] = (part1[side, other].astype(F32) + pair1[o].astype(F32)).astype(BF16)
        sum2[o] = (part2[side, other].astype(F32) + pair2[o].astype(F32)).astype(BF16)
        to = 2 * other + side
        far.append(remote(
            sum1.at[o], far1.at[o], far_send.at[0, o], far_recv.at[0, o], dp=to))
        far.append(remote(
            sum2.at[o], far2.at[o], far_send.at[1, o], far_recv.at[1, o], dp=to))
        far[-2].start()
        far[-1].start()
    landed(halo_o[2:])
    imitated[...] = convolved(grid_o, taps, rows, depth, False).astype(BF16)
    finish(halo_o)
    for copy in pair[0]:
        copy.wait()
    for copy in far:
        copy.wait()
    total1 = part1[side, level].astype(F32) + pair1[0].astype(F32)
    total2 = part2[side, level].astype(F32) + pair2[0].astype(F32)
    for o in range(1, half):
        total1 = total1 + far1[o].astype(F32)
        total2 = total2 + far2[o].astype(F32)
    grad_one[...] = total1
    grad_two[...] = total2.T

    def got_back(i, carry):
        homeward(out_b, in_b, b_send, b_recv, i).wait_recv()
        return carry

    lax.fori_loop(0, own, got_back, 0)
    feat_grad[...] = dot(back, in_b[...].reshape(slots, width)).astype(BF16)

    def drained(i, carry):
        outward(out_f, in_f, f_send, f_recv, i).wait_send()
        outward(out_g, in_g, g_send, g_recv, i).wait_send()
        homeward(out_o, in_o, o_send, o_recv, i).wait_send()
        homeward(out_b, in_b, b_send, b_recv, i).wait_send()
        return carry

    lax.fori_loop(0, own, drained, 0)


def handed_on(*refs):
    count = len(refs) // 2
    sems = refs[-1]
    copies = [
        pltpu.make_async_copy(refs[i], refs[count + i], sems.at[i]) for i in range(count)
    ]
    for copy in copies:
        copy.start()
    for copy in copies:
        copy.wait()


def per_device(feats, labels, w_first, w_second, taps, cotangent):
    n_dp = lax.axis_size("dp")
    n_ex = lax.axis_size("expert")
    rows, depth, width = feats.shape[1:]
    channels = taps.shape[2]
    hidden = w_first.shape[2]
    tokens = rows * depth
    cap = 2 * tokens // n_ex
    block = hidden // n_dp
    half = n_dp // 2
    vmem = pl.BlockSpec(memory_space=pltpu.VMEM)
    hbm = pl.BlockSpec(memory_space=pl.ANY)
    wide = pltpu.VMEM((n_ex, cap, width), BF16)
    thin = pltpu.VMEM((n_ex, cap, channels), BF16)
    grid = pltpu.VMEM((rows + 2, 3, depth, channels), BF16)
    dma = pltpu.SemaphoreType.DMA
    outs = pl.pallas_call(
        functools.partial(kernel, n_dp, n_ex),
        out_shape=(
            jax.ShapeDtypeStruct((tokens, channels), BF16),
            jax.ShapeDtypeStruct((tokens, width), BF16),
            jax.ShapeDtypeStruct((width, block), F32),
            jax.ShapeDtypeStruct((block, channels), F32),
        ),
        in_specs=[vmem, vmem, vmem, hbm, hbm, hbm],
        out_specs=(vmem,) * 4,
        scratch_shapes=[
            pltpu.VMEM((width, hidden), BF16),
            pltpu.VMEM((hidden, channels), BF16),
            pltpu.VMEM(taps.shape, BF16),
            pltpu.VMEM((n_ex, cap, tokens), BF16),
            wide, wide, thin, thin, thin, thin, wide, wide,
            pltpu.VMEM((n_ex, cap, hidden), BF16),
            pltpu.VMEM((n_ex, cap, hidden), F32),
            pltpu.VMEM((n_ex, cap, hidden), BF16),
            grid, grid,
            pltpu.VMEM((2, half, width, block), BF16),
            pltpu.VMEM((2, half, channels, block), BF16),
            pltpu.VMEM((half, width, block), BF16),
            pltpu.VMEM((half, channels, block), BF16),
            pltpu.VMEM((half, width, block), BF16),
            pltpu.VMEM((half, channels, block), BF16),
            pltpu.VMEM((half, width, block), BF16),
            pltpu.VMEM((half, channels, block), BF16),
            dma((3,)), dma((8,)), dma((8,)),
            dma((n_ex,)), dma((n_ex,)), dma((n_ex,)), dma((n_ex,)),
            dma((n_ex,)), dma((n_ex,)), dma((n_ex,)), dma((n_ex,)),
            dma((2, half)), dma((2, half)), dma((2, half)), dma((2, half)),
        ],
        compiler_params=pltpu.CompilerParams(
            collective_id=0, has_side_effects=True, vmem_limit_bytes=60 * 2**20
        ),
        name="routed_experts",
    )(
        labels.reshape(1, tokens),
        feats.reshape(tokens, width),
        cotangent.reshape(rows, depth, channels),
        w_first[0],
        w_second[0],
        taps,
    )
    imitated, feat_grad, grad_one, grad_two = pl.pallas_call(
        handed_on,
        out_shape=tuple(jax.ShapeDtypeStruct(x.shape, x.dtype) for x in outs),
        in_specs=[hbm] * 4,
        out_specs=(hbm,) * 4,
        scratch_shapes=[dma((4,))],
        compiler_params=pltpu.CompilerParams(vmem_limit_bytes=60 * 2**20),
        name="handed_on",
    )(*outs)
    return (
        imitated.reshape(1, rows, depth, channels),
        feat_grad.reshape(1, rows, depth, width),
        grad_one[None],
        grad_two[None],
    )


def solution(mesh):
    in_specs = (
        P("dp", "expert", None, None),
        P("dp", "expert", None, None),
        P("expert", None, None),
        P("expert", None, None),
        P(),
        P("dp", "expert", None, None),
    )
    out_specs = (
        P("dp", "expert", None, None),
        P("dp", "expert", None, None),
        P("expert", None, "dp"),
        P("expert", "dp", None),
    )
    return jax.shard_map(
        per_device, mesh=mesh, in_specs=in_specs, out_specs=out_specs, check_vma=False
    )
```

```python
import functools

import jax
import jax.numpy as jnp
from jax import lax
from jax.experimental import pallas as pl
from jax.experimental.pallas import tpu as pltpu
from jax.sharding import PartitionSpec as P

BF16 = jnp.bfloat16
F32 = jnp.float32
ROOT = 0.7978845608028654
CUBIC = 0.044715


def dot(a, b):
    return jnp.dot(a, b, preferred_element_type=F32)


def dot_t(a, b):
    return lax.dot_general(a, b, (((1,), (1,)), ((), ())), preferred_element_type=F32)


def remote(src, dst, send, recv, **device):
    return pltpu.make_async_remote_copy(
        src_ref=src,
        dst_ref=dst,
        send_sem=send,
        recv_sem=recv,
        device_id=device,
        device_id_type=pl.DeviceIdType.MESH,
    )


def shifted(value, step, depth):
    rows = value.shape[0]
    place = lax.broadcasted_iota(jnp.int32, value.shape, 0) % depth
    if step > 0:
        return jnp.where(place == 0, 0.0, pltpu.roll(value, 1, 0))
    return jnp.where(place == depth - 1, 0.0, pltpu.roll(value, rows - 1, 0))


def convolved(grid, taps, rows, depth, flipped):
    channels = taps.shape[1]
    tokens = rows * depth
    pieces, sums = [], []
    for a in range(3):
        for b in range(3):
            at, bt = (2 - a, 2 - b) if flipped else (a, b)
            pieces.append(grid[bt : bt + rows, at].reshape(tokens, channels))
    columns = jnp.concatenate(pieces, axis=1)
    for c in range(3):
        if flipped:
            weights = jnp.concatenate([taps[3 * k + c] for k in range(9)], axis=1)
            sums.append(dot_t(columns, weights))
        else:
            weights = jnp.concatenate([taps[3 * k + c] for k in range(9)], axis=0)
            sums.append(dot(columns, weights))
    first, last = (sums[2], sums[0]) if flipped else (sums[0], sums[2])
    return sums[1] + shifted(first, 1, depth) + shifted(last, -1, depth)


def kernel(
    n_dp, n_ex,
    labels, feats, cot, w1_hbm, w2_hbm, taps_hbm,
    imitated, feat_grad, grad_one, grad_two,
    w1, w2, taps, spread,
    out_f, in_f, out_g, in_g, out_o, in_o, out_b, in_b,
    act, slope, gate, grid_g, grid_o,
    part1, part2, pair1, pair2, sum1, sum2, far1, far2,
    load_sem, halo_send, halo_recv,
    f_send, f_recv, g_send, g_recv, o_send, o_recv, b_send, b_recv,
    pair_send, pair_recv, far_send, far_recv,
):
    tokens, width = feats.shape
    rows, depth, channels = cot.shape
    hidden = w1.shape[1]
    cap = in_f.shape[1]
    slots = n_ex * cap
    block = hidden // n_dp
    half = n_dp // 2
    dp = lax.axis_index("dp")
    me = lax.axis_index("expert")
    side = dp % 2
    level = dp // 2
    mate = dp + 1 - 2 * side

    loads = [
        pltpu.make_async_copy(w1_hbm, w1, load_sem.at[0]),
        pltpu.make_async_copy(w2_hbm, w2, load_sem.at[1]),
        pltpu.make_async_copy(taps_hbm, taps, load_sem.at[2]),
    ]
    loads[2].start()
    loads[0].start()
    loads[1].start()

    barrier = pltpu.get_barrier_semaphore()

    def greet_expert(d, carry):
        pl.semaphore_signal(
            barrier, inc=1, device_id={"expert": (me + d) % n_ex},
            device_id_type=pl.DeviceIdType.MESH,
        )
        return carry

    def greet_dp(d, carry):
        pl.semaphore_signal(
            barrier, inc=1, device_id={"dp": (dp + d) % n_dp},
            device_id_type=pl.DeviceIdType.MESH,
        )
        return carry

    lax.fori_loop(1, n_ex, greet_expert, 0)
    lax.fori_loop(1, n_dp, greet_dp, 0)
    grid_g[1 : rows + 1, 1] = cot[...]

    relative = labels[...] - me
    relative = jnp.where(relative < 0, relative + n_ex, relative)
    relative = jnp.where(
        relative >= n_ex // 2, 2 * relative - n_ex, n_ex - 1 - 2 * relative)
    named = lax.broadcasted_iota(jnp.int32, (n_ex, tokens), 0)
    hot = relative == named
    before = (
        lax.broadcasted_iota(jnp.int32, (tokens, tokens), 0)
        < lax.broadcasted_iota(jnp.int32, (tokens, tokens), 1)
    )
    rank = dot(jnp.where(hot, 1.0, 0.0).astype(BF16), jnp.where(before, 1.0, 0.0).astype(BF16))
    place = rank + (named * cap).astype(F32)
    target = jnp.sum(jnp.where(hot, place, 0.0), axis=0, keepdims=True)
    which = lax.broadcasted_iota(jnp.int32, (cap, tokens), 0)

    def halo(grid, at):
        return (
            (me < n_ex - 1, me > 0, remote(
                grid.at[rows, 1], grid.at[0, 1],
                halo_send.at[at], halo_recv.at[at], expert=(me + 1) % n_ex)),
            (me > 0, me < n_ex - 1, remote(
                grid.at[1, 1], grid.at[rows + 1, 1],
                halo_send.at[at + 1], halo_recv.at[at + 1], expert=(me + n_ex - 1) % n_ex)),
            (dp < n_dp - 1, dp > 0, remote(
                grid.at[:, 1], grid.at[:, 0],
                halo_send.at[at + 2], halo_recv.at[at + 2], dp=(dp + 1) % n_dp)),
            (dp > 0, dp < n_dp - 1, remote(
                grid.at[:, 1], grid.at[:, 2],
                halo_send.at[at + 3], halo_recv.at[at + 3], dp=(dp + n_dp - 1) % n_dp)),
        )

    def begin(steps):
        for sends, _, copy in steps:
            pl.when(sends)(copy.start)

    def landed(steps):
        for _, gets, copy in steps:
            pl.when(gets)(copy.wait_recv)

    def finish(steps):
        for sends, _, copy in steps:
            pl.when(sends)(copy.wait_send)

    def edges(grid):
        slab = jnp.zeros((rows + 2, depth, channels), BF16)
        strip = jnp.zeros((depth, channels), BF16)

        @pl.when(dp == 0)
        def _():
            grid[:, 0] = slab

        @pl.when(dp == n_dp - 1)
        def _():
            grid[:, 2] = slab

        @pl.when(me == 0)
        def _():
            grid[0, 1] = strip

        @pl.when(me == n_ex - 1)
        def _():
            grid[rows + 1, 1] = strip

    halo_g, halo_o = halo(grid_g, 0), halo(grid_o, 4)
    pl.semaphore_wait(barrier, n_ex + n_dp - 2)
    begin(halo_g[:2])

    def turn(i):
        return n_ex // 2 + (1 - 2 * (i % 2)) * ((i + 1) // 2)

    def outward(src, dst, send, recv, i):
        return remote(
            src.at[i], dst.at[i], send.at[i], recv.at[i], expert=(me + turn(i)) % n_ex
        )

    def homeward(src, dst, send, recv, i):
        return remote(
            src.at[i], dst.at[i], send.at[i], recv.at[i], expert=(me + n_ex - turn(i)) % n_ex
        )

    def chosen(i):
        hit = (which + i * cap).astype(F32) == target
        return jnp.where(hit, 1.0, 0.0).astype(BF16)

    def send_feats(i, carry):
        spread[i] = chosen(i)
        out_f[i] = dot(spread[i], feats[...]).astype(BF16)
        outward(out_f, in_f, f_send, f_recv, i).start()
        return carry

    own = n_ex - 1
    lax.fori_loop(0, 2, send_feats, 0)
    edges(grid_g)
    landed(halo_g[:2])
    begin(halo_g[2:])
    lax.fori_loop(2, own, send_feats, 0)
    spread[own] = chosen(own)
    in_f[own] = dot(spread[own], feats[...]).astype(BF16)

    tile = min(hidden, 512)
    loads[2].wait()
    landed(halo_g[2:])
    field_grad = convolved(grid_g, taps, rows, depth, True).astype(BF16)
    grid_o[1 : rows + 1, 1] = field_grad.reshape(rows, depth, channels)

    def send_grads(i, carry):
        out_g[i] = dot(spread[i], grid_o[1 : rows + 1, 1].reshape(tokens, channels)).astype(BF16)
        outward(out_g, in_g, g_send, g_recv, i).start()
        return carry

    lax.fori_loop(0, own, send_grads, 0)
    in_g[own] = dot(spread[own], grid_o[1 : rows + 1, 1].reshape(tokens, channels)).astype(BF16)
    finish(halo_g)
    loads[0].wait()
    loads[1].wait()

    def forward(k):
        both = pl.ds(2 * k, 2)
        row_block = in_f[both].reshape(2 * cap, width)
        for at in range(0, hidden, tile):
            v = dot(row_block, w1[:, at : at + tile])
            square = v * v
            t = jnp.tanh(v * (ROOT + (ROOT * CUBIC) * square))
            half_up = 0.5 + 0.5 * t
            act[both, :, at : at + tile] = (v * half_up).astype(BF16).reshape(2, cap, tile)
            inner = ROOT + (3.0 * ROOT * CUBIC) * square
            grown = half_up + (0.5 * v) * (1.0 - t * t) * inner
            slope[both, :, at : at + tile] = grown.reshape(2, cap, tile)
        result = dot(act[both].reshape(2 * cap, hidden), w2[...])
        out_o[both] = result.astype(BF16).reshape(2, cap, channels)

    def go_forward(k, carry):
        for i in (2 * k, 2 * k + 1):
            outward(out_f, in_f, f_send, f_recv, i).wait_recv()
        forward(k)
        for i in (2 * k, 2 * k + 1):
            homeward(out_o, in_o, o_send, o_recv, i).start()
        return carry

    pairs = n_ex // 2
    lax.fori_loop(0, pairs - 1, go_forward, 0)
    outward(out_f, in_f, f_send, f_recv, own - 1).wait_recv()
    forward(pairs - 1)
    homeward(out_o, in_o, o_send, o_recv, own - 1).start()
    in_o[own] = out_o[own]

    def backward(k):
        both = pl.ds(2 * k, 2)
        grads = in_g[both].reshape(2 * cap, channels)
        for at in range(0, hidden, tile):
            up = dot_t(grads, w2[at : at + tile, :])
            scale = slope[both, :, at : at + tile].reshape(2 * cap, tile)
            gate[both, :, at : at + tile] = (up * scale).astype(BF16).reshape(2, cap, tile)
        result = dot_t(gate[both].reshape(2 * cap, hidden), w1[...])
        out_b[both] = result.astype(BF16).reshape(2, cap, width)

    def got_grads(i):
        outward(out_g, in_g, g_send, g_recv, i).wait_recv()

    def send_back(i, carry):
        homeward(out_b, in_b, b_send, b_recv, i).start()
        return carry

    def go_backward(k, carry):
        got_grads(2 * k)
        got_grads(2 * k + 1)
        backward(k)
        return carry

    go_backward(0, 0)
    lax.fori_loop(0, 2, send_back, 0)
    lax.fori_loop(1, pairs - 1, go_backward, 0)
    got_grads(own - 1)
    backward(pairs - 1)
    in_b[own] = out_b[own]

    feats_t = in_f[...].reshape(slots, width).T
    grads_t = in_g[...].reshape(slots, channels).T
    pair = {}
    for o in list(range(1, half)) + [0]:
        other = (level + o) % half
        for parity in range(2):
            start = pl.multiple_of((2 * other + parity) * block, block)
            part1[parity, other] = dot(
                feats_t, gate[:, :, pl.ds(start, block)].reshape(slots, block)).astype(BF16)
            part2[parity, other] = dot(
                grads_t, act[:, :, pl.ds(start, block)].reshape(slots, block)).astype(BF16)
        pair[o] = (
            remote(part1.at[1 - side, other], pair1.at[o],
                   pair_send.at[0, o], pair_recv.at[0, o], dp=mate),
            remote(part2.at[1 - side, other], pair2.at[o],
                   pair_send.at[1, o], pair_recv.at[1, o], dp=mate),
        )
        for copy in pair[o]:
            copy.start()
    far = []
    for o in range(1, half):
        other = (level + o) % half
        for copy in pair[o]:
            copy.wait()
        sum1[o] = (part1[side, other].astype(F32) + pair1[o].astype(F32)).astype(BF16)
        sum2[o] = (part2[side, other].astype(F32) + pair2[o].astype(F32)).astype(BF16)
        to = 2 * other + side
        far.append(remote(
            sum1.at[o], far1.at[o], far_send.at[0, o], far_recv.at[0, o], dp=to))
        far.append(remote(
            sum2.at[o], far2.at[o], far_send.at[1, o], far_recv.at[1, o], dp=to))
        far[-2].start()
        far[-1].start()

    def got_outs(i, carry):
        homeward(out_o, in_o, o_send, o_recv, i).wait_recv()
        return carry

    lax.fori_loop(0, own, got_outs, 0)
    back = spread[...].reshape(slots, tokens).T
    mixed = dot(back, in_o[...].reshape(slots, channels)).astype(BF16)
    grid_o[1 : rows + 1, 1] = mixed.reshape(rows, depth, channels)
    begin(halo_o[:2])
    lax.fori_loop(2, own, send_back, 0)
    edges(grid_o)
    landed(halo_o[:2])
    begin(halo_o[2:])
    landed(halo_o[2:])
    imitated[...] = convolved(grid_o, taps, rows, depth, False).astype(BF16)
    finish(halo_o)
    for copy in pair[0]:
        copy.wait()
    for copy in far:
        copy.wait()
    total1 = part1[side, level].astype(F32) + pair1[0].astype(F32)
    total2 = part2[side, level].astype(F32) + pair2[0].astype(F32)
    for o in range(1, half):
        total1 = total1 + far1[o].astype(F32)
        total2 = total2 + far2[o].astype(F32)
    grad_one[...] = total1
    grad_two[...] = total2.T

    def got_back(i, carry):
        homeward(out_b, in_b, b_send, b_recv, i).wait_recv()
        return carry

    lax.fori_loop(0, own, got_back, 0)
    feat_grad[...] = dot(back, in_b[...].reshape(slots, width)).astype(BF16)

    def drained(i, carry):
        outward(out_f, in_f, f_send, f_recv, i).wait_send()
        outward(out_g, in_g, g_send, g_recv, i).wait_send()
        homeward(out_o, in_o, o_send, o_recv, i).wait_send()
        homeward(out_b, in_b, b_send, b_recv, i).wait_send()
        return carry

    lax.fori_loop(0, own, drained, 0)


def handed_on(*refs):
    count = len(refs) // 2
    sems = refs[-1]
    copies = [
        pltpu.make_async_copy(refs[i], refs[count + i], sems.at[i]) for i in range(count)
    ]
    for copy in copies:
        copy.start()
    for copy in copies:
        copy.wait()


def per_device(feats, labels, w_first, w_second, taps, cotangent):
    n_dp = lax.axis_size("dp")
    n_ex = lax.axis_size("expert")
    rows, depth, width = feats.shape[1:]
    channels = taps.shape[2]
    hidden = w_first.shape[2]
    tokens = rows * depth
    cap = 2 * tokens // n_ex
    block = hidden // n_dp
    half = n_dp // 2
    vmem = pl.BlockSpec(memory_space=pltpu.VMEM)
    hbm = pl.BlockSpec(memory_space=pltpu.HBM)
    wide = pltpu.VMEM((n_ex, cap, width), BF16)
    thin = pltpu.VMEM((n_ex, cap, channels), BF16)
    grid = pltpu.VMEM((rows + 2, 3, depth, channels), BF16)
    dma = pltpu.SemaphoreType.DMA
    outs = pl.pallas_call(
        functools.partial(kernel, n_dp, n_ex),
        out_shape=(
            jax.ShapeDtypeStruct((tokens, channels), BF16),
            jax.ShapeDtypeStruct((tokens, width), BF16),
            jax.ShapeDtypeStruct((width, block), F32),
            jax.ShapeDtypeStruct((block, channels), F32),
        ),
        in_specs=[vmem, vmem, vmem, hbm, hbm, hbm],
        out_specs=(vmem,) * 4,
        scratch_shapes=[
            pltpu.VMEM((width, hidden), BF16),
            pltpu.VMEM((hidden, channels), BF16),
            pltpu.VMEM(taps.shape, BF16),
            pltpu.VMEM((n_ex, cap, tokens), BF16),
            wide, wide, thin, thin, thin, thin, wide, wide,
            pltpu.VMEM((n_ex, cap, hidden), BF16),
            pltpu.VMEM((n_ex, cap, hidden), F32),
            pltpu.VMEM((n_ex, cap, hidden), BF16),
            grid, grid,
            pltpu.VMEM((2, half, width, block), BF16),
            pltpu.VMEM((2, half, channels, block), BF16),
            pltpu.VMEM((half, width, block), BF16),
            pltpu.VMEM((half, channels, block), BF16),
            pltpu.VMEM((half, width, block), BF16),
            pltpu.VMEM((half, channels, block), BF16),
            pltpu.VMEM((half, width, block), BF16),
            pltpu.VMEM((half, channels, block), BF16),
            dma((3,)), dma((8,)), dma((8,)),
            dma((n_ex,)), dma((n_ex,)), dma((n_ex,)), dma((n_ex,)),
            dma((n_ex,)), dma((n_ex,)), dma((n_ex,)), dma((n_ex,)),
            dma((2, half)), dma((2, half)), dma((2, half)), dma((2, half)),
        ],
        compiler_params=pltpu.CompilerParams(
            collective_id=0, has_side_effects=True, vmem_limit_bytes=50 * 2**20
        ),
        name="routed_experts",
    )(
        labels.reshape(1, tokens),
        feats.reshape(tokens, width),
        cotangent.reshape(rows, depth, channels),
        w_first[0],
        w_second[0],
        taps,
    )
    imitated, feat_grad, grad_one, grad_two = pl.pallas_call(
        handed_on,
        out_shape=tuple(jax.ShapeDtypeStruct(x.shape, x.dtype) for x in outs),
        in_specs=[vmem] * 4,
        out_specs=(hbm,) * 4,
        scratch_shapes=[dma((4,))],
        compiler_params=pltpu.CompilerParams(vmem_limit_bytes=8 * 2**20),
        name="handed_on",
    )(*outs)
    return (
        imitated.reshape(1, rows, depth, channels),
        feat_grad.reshape(1, rows, depth, width),
        grad_one[None],
        grad_two[None],
    )


def solution(mesh):
    in_specs = (
        P("dp", "expert", None, None),
        P("dp", "expert", None, None),
        P("expert", None, None),
        P("expert", None, None),
        P(),
        P("dp", "expert", None, None),
    )
    out_specs = (
        P("dp", "expert", None, None),
        P("dp", "expert", None, None),
        P("expert", None, "dp"),
        P("expert", "dp", None),
    )
    return jax.shard_map(
        per_device, mesh=mesh, in_specs=in_specs, out_specs=out_specs, check_vma=False
    )
```

```python
import functools

import jax
import jax.numpy as jnp
from jax import lax
from jax.experimental import pallas as pl
from jax.experimental.pallas import tpu as pltpu
from jax.sharding import PartitionSpec as P

BF16 = jnp.bfloat16
F32 = jnp.float32
ROOT = 0.7978845608028654
CUBIC = 0.044715


def dot(a, b):
    return jnp.dot(a, b, preferred_element_type=F32)


def dot_t(a, b):
    return lax.dot_general(a, b, (((1,), (1,)), ((), ())), preferred_element_type=F32)


def remote(src, dst, send, recv, **device):
    return pltpu.make_async_remote_copy(
        src_ref=src,
        dst_ref=dst,
        send_sem=send,
        recv_sem=recv,
        device_id=device,
        device_id_type=pl.DeviceIdType.MESH,
    )


def shifted(value, step, depth):
    rows = value.shape[0]
    place = lax.broadcasted_iota(jnp.int32, value.shape, 0) % depth
    if step > 0:
        return jnp.where(place == 0, 0.0, pltpu.roll(value, 1, 0))
    return jnp.where(place == depth - 1, 0.0, pltpu.roll(value, rows - 1, 0))


def convolved(grid, taps, rows, depth, flipped):
    channels = taps.shape[1]
    tokens = rows * depth
    pieces, sums = [], []
    for a in range(3):
        for b in range(3):
            at, bt = (2 - a, 2 - b) if flipped else (a, b)
            pieces.append(grid[bt : bt + rows, at].reshape(tokens, channels))
    columns = jnp.concatenate(pieces, axis=1)
    for c in range(3):
        if flipped:
            weights = jnp.concatenate([taps[3 * k + c] for k in range(9)], axis=1)
            sums.append(dot_t(columns, weights))
        else:
            weights = jnp.concatenate([taps[3 * k + c] for k in range(9)], axis=0)
            sums.append(dot(columns, weights))
    first, last = (sums[2], sums[0]) if flipped else (sums[0], sums[2])
    return sums[1] + shifted(first, 1, depth) + shifted(last, -1, depth)


def kernel(
    n_dp, n_ex,
    labels_hbm, feats_hbm, cot_hbm, w1_hbm, w2_hbm, taps_hbm,
    imitated_hbm, feat_grad_hbm, grad_one_hbm, grad_two_hbm,
    imitated, feat_grad, grad_one, grad_two,
    labels, feats, w1, w2, taps, spread,
    out_f, in_f, out_g, in_g, out_o, in_o, out_b, in_b,
    act, slope, gate, grid_g, grid_o,
    part1, part2, pair1, pair2, sum1, sum2, far1, far2,
    load_sem, store_sem, halo_send, halo_recv,
    f_send, f_recv, g_send, g_recv, o_send, o_recv, b_send, b_recv,
    pair_send, pair_recv, far_send, far_recv,
):
    tokens, width = feats.shape
    rows, depth, channels = cot_hbm.shape
    hidden = w1.shape[1]
    cap = in_f.shape[1]
    slots = n_ex * cap
    block = hidden // n_dp
    half = n_dp // 2
    dp = lax.axis_index("dp")
    me = lax.axis_index("expert")
    side = dp % 2
    level = dp // 2
    mate = dp + 1 - 2 * side

    loads = [
        pltpu.make_async_copy(w1_hbm, w1, load_sem.at[0]),
        pltpu.make_async_copy(w2_hbm, w2, load_sem.at[1]),
        pltpu.make_async_copy(taps_hbm, taps, load_sem.at[2]),
        pltpu.make_async_copy(labels_hbm, labels, load_sem.at[3]),
        pltpu.make_async_copy(cot_hbm, grid_g.at[pl.ds(1, rows), 1], load_sem.at[4]),
        pltpu.make_async_copy(feats_hbm, feats, load_sem.at[5]),
    ]
    for at in (3, 4, 5, 2, 0, 1):
        loads[at].start()

    stores = [
        pltpu.make_async_copy(imitated, imitated_hbm, store_sem.at[0]),
        pltpu.make_async_copy(grad_one, grad_one_hbm, store_sem.at[1]),
        pltpu.make_async_copy(grad_two, grad_two_hbm, store_sem.at[2]),
        pltpu.make_async_copy(feat_grad, feat_grad_hbm, store_sem.at[3]),
    ]

    barrier = pltpu.get_barrier_semaphore()

    def greet_expert(d, carry):
        pl.semaphore_signal(
            barrier, inc=1, device_id={"expert": (me + d) % n_ex},
            device_id_type=pl.DeviceIdType.MESH,
        )
        return carry

    def greet_dp(d, carry):
        pl.semaphore_signal(
            barrier, inc=1, device_id={"dp": (dp + d) % n_dp},
            device_id_type=pl.DeviceIdType.MESH,
        )
        return carry

    lax.fori_loop(1, n_ex, greet_expert, 0)
    lax.fori_loop(1, n_dp, greet_dp, 0)
    loads[3].wait()

    relative = labels[...] - me
    relative = jnp.where(relative < 0, relative + n_ex, relative)
    relative = jnp.where(
        relative >= n_ex // 2, 2 * relative - n_ex, n_ex - 1 - 2 * relative)
    named = lax.broadcasted_iota(jnp.int32, (n_ex, tokens), 0)
    hot = relative == named
    before = (
        lax.broadcasted_iota(jnp.int32, (tokens, tokens), 0)
        < lax.broadcasted_iota(jnp.int32, (tokens, tokens), 1)
    )
    rank = dot(jnp.where(hot, 1.0, 0.0).astype(BF16), jnp.where(before, 1.0, 0.0).astype(BF16))
    place = rank + (named * cap).astype(F32)
    target = jnp.sum(jnp.where(hot, place, 0.0), axis=0, keepdims=True)
    which = lax.broadcasted_iota(jnp.int32, (cap, tokens), 0)

    def halo(grid, at):
        return (
            (me < n_ex - 1, me > 0, remote(
                grid.at[rows, 1], grid.at[0, 1],
                halo_send.at[at], halo_recv.at[at], expert=(me + 1) % n_ex)),
            (me > 0, me < n_ex - 1, remote(
                grid.at[1, 1], grid.at[rows + 1, 1],
                halo_send.at[at + 1], halo_recv.at[at + 1], expert=(me + n_ex - 1) % n_ex)),
            (dp < n_dp - 1, dp > 0, remote(
                grid.at[:, 1], grid.at[:, 0],
                halo_send.at[at + 2], halo_recv.at[at + 2], dp=(dp + 1) % n_dp)),
            (dp > 0, dp < n_dp - 1, remote(
                grid.at[:, 1], grid.at[:, 2],
                halo_send.at[at + 3], halo_recv.at[at + 3], dp=(dp + n_dp - 1) % n_dp)),
        )

    def begin(steps):
        for sends, _, copy in steps:
            pl.when(sends)(copy.start)

    def landed(steps):
        for _, gets, copy in steps:
            pl.when(gets)(copy.wait_recv)

    def finish(steps):
        for sends, _, copy in steps:
            pl.when(sends)(copy.wait_send)

    def edges(grid):
        slab = jnp.zeros((rows + 2, depth, channels), BF16)
        strip = jnp.zeros((depth, channels), BF16)

        @pl.when(dp == 0)
        def _():
            grid[:, 0] = slab

        @pl.when(dp == n_dp - 1)
        def _():
            grid[:, 2] = slab

        @pl.when(me == 0)
        def _():
            grid[0, 1] = strip

        @pl.when(me == n_ex - 1)
        def _():
            grid[rows + 1, 1] = strip

    halo_g, halo_o = halo(grid_g, 0), halo(grid_o, 4)
    loads[4].wait()
    pl.semaphore_wait(barrier, n_ex + n_dp - 2)
    begin(halo_g[:2])
    loads[5].wait()

    def turn(i):
        return n_ex // 2 + (1 - 2 * (i % 2)) * ((i + 1) // 2)

    def outward(src, dst, send, recv, i):
        return remote(
            src.at[i], dst.at[i], send.at[i], recv.at[i], expert=(me + turn(i)) % n_ex
        )

    def homeward(src, dst, send, recv, i):
        return remote(
            src.at[i], dst.at[i], send.at[i], recv.at[i], expert=(me + n_ex - turn(i)) % n_ex
        )

    def chosen(i):
        hit = (which + i * cap).astype(F32) == target
        return jnp.where(hit, 1.0, 0.0).astype(BF16)

    def send_feats(i, carry):
        spread[i] = chosen(i)
        out_f[i] = dot(spread[i], feats[...]).astype(BF16)
        outward(out_f, in_f, f_send, f_recv, i).start()
        return carry

    own = n_ex - 1
    lax.fori_loop(0, 2, send_feats, 0)
    edges(grid_g)
    landed(halo_g[:2])
    begin(halo_g[2:])
    lax.fori_loop(2, own, send_feats, 0)
    spread[own] = chosen(own)
    in_f[own] = dot(spread[own], feats[...]).astype(BF16)

    tile = min(hidden, 512)
    loads[2].wait()
    landed(halo_g[2:])
    field_grad = convolved(grid_g, taps, rows, depth, True).astype(BF16)
    grid_o[1 : rows + 1, 1] = field_grad.reshape(rows, depth, channels)

    def send_grads(i, carry):
        out_g[i] = dot(spread[i], grid_o[1 : rows + 1, 1].reshape(tokens, channels)).astype(BF16)
        outward(out_g, in_g, g_send, g_recv, i).start()
        return carry

    lax.fori_loop(0, own, send_grads, 0)
    in_g[own] = dot(spread[own], grid_o[1 : rows + 1, 1].reshape(tokens, channels)).astype(BF16)
    finish(halo_g)
    loads[0].wait()
    loads[1].wait()

    def forward(k):
        both = pl.ds(2 * k, 2)
        row_block = in_f[both].reshape(2 * cap, width)
        for at in range(0, hidden, tile):
            v = dot(row_block, w1[:, at : at + tile])
            square = v * v
            t = jnp.tanh(v * (ROOT + (ROOT * CUBIC) * square))
            half_up = 0.5 + 0.5 * t
            act[both, :, at : at + tile] = (v * half_up).astype(BF16).reshape(2, cap, tile)
            inner = ROOT + (3.0 * ROOT * CUBIC) * square
            grown = half_up + (0.5 * v) * (1.0 - t * t) * inner
            slope[both, :, at : at + tile] = grown.reshape(2, cap, tile)
        result = dot(act[both].reshape(2 * cap, hidden), w2[...])
        out_o[both] = result.astype(BF16).reshape(2, cap, channels)

    def go_forward(k, carry):
        for i in (2 * k, 2 * k + 1):
            outward(out_f, in_f, f_send, f_recv, i).wait_recv()
        forward(k)
        return carry

    pairs = n_ex // 2
    lax.fori_loop(0, pairs - 1, go_forward, 0)
    outward(out_f, in_f, f_send, f_recv, own - 1).wait_recv()
    forward(pairs - 1)
    in_o[own] = out_o[own]

    def backward(k):
        both = pl.ds(2 * k, 2)
        grads = in_g[both].reshape(2 * cap, channels)
        for at in range(0, hidden, tile):
            up = dot_t(grads, w2[at : at + tile, :])
            scale = slope[both, :, at : at + tile].reshape(2 * cap, tile)
            gate[both, :, at : at + tile] = (up * scale).astype(BF16).reshape(2, cap, tile)
        result = dot_t(gate[both].reshape(2 * cap, hidden), w1[...])
        out_b[both] = result.astype(BF16).reshape(2, cap, width)

    def got_grads(i):
        outward(out_g, in_g, g_send, g_recv, i).wait_recv()

    def send_back(i, carry):
        homeward(out_b, in_b, b_send, b_recv, i).start()
        return carry

    def go_backward(k, carry):
        got_grads(2 * k)
        got_grads(2 * k + 1)
        backward(k)
        return carry

    def send_outs(i, carry):
        homeward(out_o, in_o, o_send, o_recv, i).start()
        return carry

    got_grads(0)
    got_grads(1)
    lax.fori_loop(0, own, send_outs, 0)
    backward(0)
    lax.fori_loop(0, 2, send_back, 0)
    lax.fori_loop(1, pairs // 2, go_backward, 0)
    lax.fori_loop(2, pairs, send_back, 0)
    lax.fori_loop(pairs // 2, pairs - 1, go_backward, 0)
    got_grads(own - 1)
    backward(pairs - 1)
    in_b[own] = out_b[own]

    feats_t = in_f[...].reshape(slots, width).T
    grads_t = in_g[...].reshape(slots, channels).T
    pair = {}

    def weight_blocks(o):
        other = (level + o) % half
        for parity in range(2):
            start = pl.multiple_of((2 * other + parity) * block, block)
            part1[parity, other] = dot(
                feats_t, gate[:, :, pl.ds(start, block)].reshape(slots, block)).astype(BF16)
            part2[parity, other] = dot(
                grads_t, act[:, :, pl.ds(start, block)].reshape(slots, block)).astype(BF16)
        pair[o] = (
            remote(part1.at[1 - side, other], pair1.at[o],
                   pair_send.at[0, o], pair_recv.at[0, o], dp=mate),
            remote(part2.at[1 - side, other], pair2.at[o],
                   pair_send.at[1, o], pair_recv.at[1, o], dp=mate),
        )
        for copy in pair[o]:
            copy.start()

    def got_outs(i, carry):
        homeward(out_o, in_o, o_send, o_recv, i).wait_recv()
        return carry

    for o in range(1, half):
        weight_blocks(o)
    lax.fori_loop(0, own, got_outs, 0)
    back = spread[...].reshape(slots, tokens).T
    mixed = dot(back, in_o[...].reshape(slots, channels)).astype(BF16)
    grid_o[1 : rows + 1, 1] = mixed.reshape(rows, depth, channels)
    begin(halo_o[:2])
    lax.fori_loop(pairs, own, send_back, 0)
    edges(grid_o)
    weight_blocks(0)
    landed(halo_o[:2])
    begin(halo_o[2:])
    far = []
    for o in range(1, half):
        other = (level + o) % half
        for copy in pair[o]:
            copy.wait()
        sum1[o] = (part1[side, other].astype(F32) + pair1[o].astype(F32)).astype(BF16)
        sum2[o] = (part2[side, other].astype(F32) + pair2[o].astype(F32)).astype(BF16)
        to = 2 * other + side
        far.append(remote(
            sum1.at[o], far1.at[o], far_send.at[0, o], far_recv.at[0, o], dp=to))
        far.append(remote(
            sum2.at[o], far2.at[o], far_send.at[1, o], far_recv.at[1, o], dp=to))
        far[-2].start()
        far[-1].start()
    landed(halo_o[2:])
    imitated[...] = convolved(grid_o, taps, rows, depth, False).astype(BF16)
    stores[0].start()
    finish(halo_o)
    for copy in pair[0]:
        copy.wait()
    for copy in far:
        copy.wait()
    total1 = part1[side, level].astype(F32) + pair1[0].astype(F32)
    total2 = part2[side, level].astype(F32) + pair2[0].astype(F32)
    for o in range(1, half):
        total1 = total1 + far1[o].astype(F32)
        total2 = total2 + far2[o].astype(F32)
    grad_one[...] = total1
    grad_two[...] = total2.T
    stores[1].start()
    stores[2].start()

    def got_back(i, carry):
        homeward(out_b, in_b, b_send, b_recv, i).wait_recv()
        return carry

    lax.fori_loop(0, pairs, got_back, 0)
    middle = pairs * cap
    early = dot(back[:, :middle], in_b[:pairs].reshape(middle, width))
    lax.fori_loop(pairs, own, got_back, 0)
    late = dot(back[:, middle:], in_b[pairs:].reshape(middle, width))
    feat_grad[...] = (early + late).astype(BF16)
    stores[3].start()

    def drained(i, carry):
        outward(out_f, in_f, f_send, f_recv, i).wait_send()
        outward(out_g, in_g, g_send, g_recv, i).wait_send()
        homeward(out_o, in_o, o_send, o_recv, i).wait_send()
        homeward(out_b, in_b, b_send, b_recv, i).wait_send()
        return carry

    lax.fori_loop(0, own, drained, 0)
    for copy in stores:
        copy.wait()


def handed_on(*refs):
    count = (len(refs) - 2) // 3
    news, olds, held = refs[count : 2 * count], refs[:count], refs[2 * count : 3 * count]
    in_sem, out_sem = refs[-2:]
    reads = [pltpu.make_async_copy(olds[i], held[i], in_sem.at[i]) for i in range(count)]
    writes = [pltpu.make_async_copy(held[i], news[i], out_sem.at[i]) for i in range(count)]
    for copy in reads:
        copy.start()
    for read, write in zip(reads, writes):
        read.wait()
        write.start()
    for copy in writes:
        copy.wait()


def per_device(feats, labels, w_first, w_second, taps, cotangent):
    n_dp = lax.axis_size("dp")
    n_ex = lax.axis_size("expert")
    rows, depth, width = feats.shape[1:]
    channels = taps.shape[2]
    hidden = w_first.shape[2]
    tokens = rows * depth
    cap = 2 * tokens // n_ex
    block = hidden // n_dp
    half = n_dp // 2
    hbm = pl.BlockSpec(memory_space=pltpu.HBM)
    wide = pltpu.VMEM((n_ex, cap, width), BF16)
    thin = pltpu.VMEM((n_ex, cap, channels), BF16)
    grid = pltpu.VMEM((rows + 2, 3, depth, channels), BF16)
    dma = pltpu.SemaphoreType.DMA
    outs = pl.pallas_call(
        functools.partial(kernel, n_dp, n_ex),
        out_shape=(
            jax.ShapeDtypeStruct((tokens, channels), BF16),
            jax.ShapeDtypeStruct((tokens, width), BF16),
            jax.ShapeDtypeStruct((width, block), F32),
            jax.ShapeDtypeStruct((block, channels), F32),
        ),
        in_specs=[hbm] * 6,
        out_specs=(hbm,) * 4,
        scratch_shapes=[
            pltpu.VMEM((tokens, channels), BF16),
            pltpu.VMEM((tokens, width), BF16),
            pltpu.VMEM((width, block), F32),
            pltpu.VMEM((block, channels), F32),
            pltpu.VMEM((1, tokens), jnp.int32),
            pltpu.VMEM((tokens, width), BF16),
            pltpu.VMEM((width, hidden), BF16),
            pltpu.VMEM((hidden, channels), BF16),
            pltpu.VMEM(taps.shape, BF16),
            pltpu.VMEM((n_ex, cap, tokens), BF16),
            wide, wide, thin, thin, thin, thin, wide, wide,
            pltpu.VMEM((n_ex, cap, hidden), BF16),
            pltpu.VMEM((n_ex, cap, hidden), F32),
            pltpu.VMEM((n_ex, cap, hidden), BF16),
            grid, grid,
            pltpu.VMEM((2, half, width, block), BF16),
            pltpu.VMEM((2, half, channels, block), BF16),
            pltpu.VMEM((half, width, block), BF16),
            pltpu.VMEM((half, channels, block), BF16),
            pltpu.VMEM((half, width, block), BF16),
            pltpu.VMEM((half, channels, block), BF16),
            pltpu.VMEM((half, width, block), BF16),
            pltpu.VMEM((half, channels, block), BF16),
            dma((6,)), dma((4,)), dma((8,)), dma((8,)),
            dma((n_ex,)), dma((n_ex,)), dma((n_ex,)), dma((n_ex,)),
            dma((n_ex,)), dma((n_ex,)), dma((n_ex,)), dma((n_ex,)),
            dma((2, half)), dma((2, half)), dma((2, half)), dma((2, half)),
        ],
        compiler_params=pltpu.CompilerParams(
            collective_id=0, has_side_effects=True, vmem_limit_bytes=60 * 2**20
        ),
        name="routed_experts",
    )(
        labels.reshape(1, tokens),
        feats.reshape(tokens, width),
        cotangent.reshape(rows, depth, channels),
        w_first[0],
        w_second[0],
        taps,
    )
    imitated, feat_grad, grad_one, grad_two = pl.pallas_call(
        handed_on,
        out_shape=tuple(jax.ShapeDtypeStruct(x.shape, x.dtype) for x in outs),
        in_specs=[hbm] * 4,
        out_specs=(hbm,) * 4,
        scratch_shapes=[pltpu.VMEM(x.shape, x.dtype) for x in outs] + [dma((4,)), dma((4,))],
        compiler_params=pltpu.CompilerParams(vmem_limit_bytes=60 * 2**20),
        name="handed_on",
    )(*outs)
    return (
        imitated.reshape(1, rows, depth, channels),
        feat_grad.reshape(1, rows, depth, width),
        grad_one[None],
        grad_two[None],
    )


def solution(mesh):
    in_specs = (
        P("dp", "expert", None, None),
        P("dp", "expert", None, None),
        P("expert", None, None),
        P("expert", None, None),
        P(),
        P("dp", "expert", None, None),
    )
    out_specs = (
        P("dp", "expert", None, None),
        P("dp", "expert", None, None),
        P("expert", None, "dp"),
        P("expert", "dp", None),
    )
    return jax.shard_map(
        per_device, mesh=mesh, in_specs=in_specs, out_specs=out_specs, check_vma=False
    )
```

```python
import functools

import jax
import jax.numpy as jnp
from jax import lax
from jax.experimental import pallas as pl
from jax.experimental.pallas import tpu as pltpu
from jax.sharding import PartitionSpec as P

BF16 = jnp.bfloat16
F32 = jnp.float32
ROOT = 0.7978845608028654
CUBIC = 0.044715


def dot(a, b):
    return jnp.dot(a, b, preferred_element_type=F32)


def dot_t(a, b):
    return lax.dot_general(a, b, (((1,), (1,)), ((), ())), preferred_element_type=F32)


def remote(src, dst, send, recv, **device):
    return pltpu.make_async_remote_copy(
        src_ref=src,
        dst_ref=dst,
        send_sem=send,
        recv_sem=recv,
        device_id=device,
        device_id_type=pl.DeviceIdType.MESH,
    )


def shifted(value, step, depth):
    rows = value.shape[0]
    place = lax.broadcasted_iota(jnp.int32, value.shape, 0) % depth
    if step > 0:
        return jnp.where(place == 0, 0.0, pltpu.roll(value, 1, 0))
    return jnp.where(place == depth - 1, 0.0, pltpu.roll(value, rows - 1, 0))


def convolved(grid, taps, rows, depth, flipped):
    channels = taps.shape[1]
    tokens = rows * depth
    pieces, sums = [], []
    for a in range(3):
        for b in range(3):
            at, bt = (2 - a, 2 - b) if flipped else (a, b)
            pieces.append(grid[bt : bt + rows, at].reshape(tokens, channels))
    columns = jnp.concatenate(pieces, axis=1)
    for c in range(3):
        if flipped:
            weights = jnp.concatenate([taps[3 * k + c] for k in range(9)], axis=1)
            sums.append(dot_t(columns, weights))
        else:
            weights = jnp.concatenate([taps[3 * k + c] for k in range(9)], axis=0)
            sums.append(dot(columns, weights))
    first, last = (sums[2], sums[0]) if flipped else (sums[0], sums[2])
    return sums[1] + shifted(first, 1, depth) + shifted(last, -1, depth)


def kernel(
    n_dp, n_ex,
    labels_hbm, feats_hbm, cot_hbm, w1_hbm, w2_hbm, taps_hbm,
    imitated_hbm, feat_grad_hbm, grad_one_hbm, grad_two_hbm,
    imitated, feat_grad, grad_one, grad_two,
    labels, feats, w1, w2, taps, spread,
    out_f, in_f, out_g, in_g, out_o, in_o, out_b, in_b,
    act, slope, gate, grid_g, grid_o,
    part1, part2, pair1, pair2, sum1, sum2, far1, far2,
    load_sem, store_sem, halo_send, halo_recv,
    f_send, f_recv, g_send, g_recv, o_send, o_recv, b_send, b_recv,
    pair_send, pair_recv, far_send, far_recv,
):
    tokens, width = feats.shape
    rows, depth, channels = cot_hbm.shape
    hidden = w1.shape[1]
    cap = in_f.shape[1]
    slots = n_ex * cap
    block = hidden // n_dp
    half = n_dp // 2
    dp = lax.axis_index("dp")
    me = lax.axis_index("expert")
    side = dp % 2
    level = dp // 2
    mate = dp + 1 - 2 * side

    loads = [
        pltpu.make_async_copy(w1_hbm, w1, load_sem.at[0]),
        pltpu.make_async_copy(w2_hbm, w2, load_sem.at[1]),
        pltpu.make_async_copy(taps_hbm, taps, load_sem.at[2]),
        pltpu.make_async_copy(labels_hbm, labels, load_sem.at[3]),
        pltpu.make_async_copy(cot_hbm, grid_g.at[pl.ds(1, rows), 1], load_sem.at[4]),
        pltpu.make_async_copy(feats_hbm, feats, load_sem.at[5]),
    ]
    for at in (3, 4, 5, 2, 0, 1):
        loads[at].start()

    stores = [
        pltpu.make_async_copy(imitated, imitated_hbm, store_sem.at[0]),
        pltpu.make_async_copy(grad_one, grad_one_hbm, store_sem.at[1]),
        pltpu.make_async_copy(grad_two, grad_two_hbm, store_sem.at[2]),
        pltpu.make_async_copy(feat_grad, feat_grad_hbm, store_sem.at[3]),
    ]

    barrier = pltpu.get_barrier_semaphore()

    def greet_expert(d, carry):
        pl.semaphore_signal(
            barrier, inc=1, device_id={"expert": (me + d) % n_ex},
            device_id_type=pl.DeviceIdType.MESH,
        )
        return carry

    def greet_dp(d, carry):
        pl.semaphore_signal(
            barrier, inc=1, device_id={"dp": (dp + d) % n_dp},
            device_id_type=pl.DeviceIdType.MESH,
        )
        return carry

    for x in (1, n_dp - 1):
        for y in (1, n_ex - 1):
            pl.semaphore_signal(
                barrier, inc=1,
                device_id={"dp": (dp + x) % n_dp, "expert": (me + y) % n_ex},
                device_id_type=pl.DeviceIdType.MESH,
            )
    lax.fori_loop(1, n_ex, greet_expert, 0)
    lax.fori_loop(1, n_dp, greet_dp, 0)
    loads[3].wait()

    relative = labels[...] - me
    relative = jnp.where(relative < 0, relative + n_ex, relative)
    relative = jnp.where(
        relative >= n_ex // 2, 2 * relative - n_ex, n_ex - 1 - 2 * relative)
    named = lax.broadcasted_iota(jnp.int32, (n_ex, tokens), 0)
    hot = relative == named
    before = (
        lax.broadcasted_iota(jnp.int32, (tokens, tokens), 0)
        < lax.broadcasted_iota(jnp.int32, (tokens, tokens), 1)
    )
    rank = dot(jnp.where(hot, 1.0, 0.0).astype(BF16), jnp.where(before, 1.0, 0.0).astype(BF16))
    place = rank + (named * cap).astype(F32)
    target = jnp.sum(jnp.where(hot, place, 0.0), axis=0, keepdims=True)
    which = lax.broadcasted_iota(jnp.int32, (cap, tokens), 0)

    def halo(grid, at):
        return (
            (me < n_ex - 1, me > 0, remote(
                grid.at[rows, 1], grid.at[0, 1],
                halo_send.at[at], halo_recv.at[at], expert=(me + 1) % n_ex)),
            (me > 0, me < n_ex - 1, remote(
                grid.at[1, 1], grid.at[rows + 1, 1],
                halo_send.at[at + 1], halo_recv.at[at + 1], expert=(me + n_ex - 1) % n_ex)),
            (dp < n_dp - 1, dp > 0, remote(
                grid.at[:, 1], grid.at[:, 0],
                halo_send.at[at + 2], halo_recv.at[at + 2], dp=(dp + 1) % n_dp)),
            (dp > 0, dp < n_dp - 1, remote(
                grid.at[:, 1], grid.at[:, 2],
                halo_send.at[at + 3], halo_recv.at[at + 3], dp=(dp + n_dp - 1) % n_dp)),
        )

    def begin(steps):
        for sends, _, copy in steps:
            pl.when(sends)(copy.start)

    def landed(steps):
        for _, gets, copy in steps:
            pl.when(gets)(copy.wait_recv)

    def finish(steps):
        for sends, _, copy in steps:
            pl.when(sends)(copy.wait_send)

    def edges(grid):
        slab = jnp.zeros((rows + 2, depth, channels), BF16)
        strip = jnp.zeros((depth, channels), BF16)

        @pl.when(dp == 0)
        def _():
            grid[:, 0] = slab

        @pl.when(dp == n_dp - 1)
        def _():
            grid[:, 2] = slab

        @pl.when(me == 0)
        def _():
            grid[0, 1] = strip

        @pl.when(me == n_ex - 1)
        def _():
            grid[rows + 1, 1] = strip

    def halo_at_once(grid, at):
        inner = pl.ds(1, rows)
        steps = []
        for x in (-1, 0, 1):
            for y in (-1, 0, 1):
                if x == 0 and y == 0:
                    continue
                mine = {-1: 1, 0: inner, 1: rows}[y]
                theirs = {-1: rows + 1, 0: inner, 1: 0}[y]
                near = True
                come = True
                if x != 0:
                    near = dp < n_dp - 1 if x > 0 else dp > 0
                    come = dp > 0 if x > 0 else dp < n_dp - 1
                if y != 0:
                    goes = me < n_ex - 1 if y > 0 else me > 0
                    gets = me > 0 if y > 0 else me < n_ex - 1
                    near = goes if x == 0 else jnp.logical_and(near, goes)
                    come = gets if x == 0 else jnp.logical_and(come, gets)
                spot = at + len(steps)
                steps.append((near, come, remote(
                    grid.at[mine, 1], grid.at[theirs, 1 - x],
                    halo_send.at[spot], halo_recv.at[spot],
                    dp=(dp + x + n_dp) % n_dp, expert=(me + y + n_ex) % n_ex)))
        return steps

    halo_g, halo_o = halo(grid_g, 0), halo_at_once(grid_o, 4)
    loads[4].wait()
    pl.semaphore_wait(barrier, n_ex + n_dp + 2)
    begin(halo_g[:2])
    loads[5].wait()

    def turn(i):
        return n_ex // 2 + (1 - 2 * (i % 2)) * ((i + 1) // 2)

    def outward(src, dst, send, recv, i):
        return remote(
            src.at[i], dst.at[i], send.at[i], recv.at[i], expert=(me + turn(i)) % n_ex
        )

    def homeward(src, dst, send, recv, i):
        return remote(
            src.at[i], dst.at[i], send.at[i], recv.at[i], expert=(me + n_ex - turn(i)) % n_ex
        )

    def chosen(i):
        hit = (which + i * cap).astype(F32) == target
        return jnp.where(hit, 1.0, 0.0).astype(BF16)

    def send_feats(i, carry):
        spread[i] = chosen(i)
        out_f[i] = dot(spread[i], feats[...]).astype(BF16)
        outward(out_f, in_f, f_send, f_recv, i).start()
        return carry

    own = n_ex - 1
    lax.fori_loop(0, 2, send_feats, 0)
    edges(grid_g)
    edges(grid_o)
    strips = jnp.zeros((3, depth, channels), BF16)

    @pl.when(me == 0)
    def _():
        grid_o[0] = strips

    @pl.when(me == n_ex - 1)
    def _():
        grid_o[rows + 1] = strips

    landed(halo_g[:2])
    begin(halo_g[2:])
    lax.fori_loop(2, own, send_feats, 0)
    spread[own] = chosen(own)
    in_f[own] = dot(spread[own], feats[...]).astype(BF16)

    tile = min(hidden, 512)
    loads[2].wait()
    landed(halo_g[2:])
    field_grad = convolved(grid_g, taps, rows, depth, True).astype(BF16)
    grid_o[1 : rows + 1, 1] = field_grad.reshape(rows, depth, channels)

    def send_grads(i, carry):
        out_g[i] = dot(spread[i], grid_o[1 : rows + 1, 1].reshape(tokens, channels)).astype(BF16)
        outward(out_g, in_g, g_send, g_recv, i).start()
        return carry

    lax.fori_loop(0, own, send_grads, 0)
    in_g[own] = dot(spread[own], grid_o[1 : rows + 1, 1].reshape(tokens, channels)).astype(BF16)
    finish(halo_g)
    loads[0].wait()
    loads[1].wait()

    def forward(k):
        both = pl.ds(2 * k, 2)
        row_block = in_f[both].reshape(2 * cap, width)
        for at in range(0, hidden, tile):
            v = dot(row_block, w1[:, at : at + tile])
            square = v * v
            t = jnp.tanh(v * (ROOT + (ROOT * CUBIC) * square))
            half_up = 0.5 + 0.5 * t
            act[both, :, at : at + tile] = (v * half_up).astype(BF16).reshape(2, cap, tile)
            inner = ROOT + (3.0 * ROOT * CUBIC) * square
            grown = half_up + (0.5 * v) * (1.0 - t * t) * inner
            slope[both, :, at : at + tile] = grown.reshape(2, cap, tile)
        result = dot(act[both].reshape(2 * cap, hidden), w2[...])
        out_o[both] = result.astype(BF16).reshape(2, cap, channels)

    def go_forward(k, carry):
        for i in (2 * k, 2 * k + 1):
            outward(out_f, in_f, f_send, f_recv, i).wait_recv()
        forward(k)
        for i in (2 * k, 2 * k + 1):
            homeward(out_o, in_o, o_send, o_recv, i).start()
        return carry

    pairs = n_ex // 2
    lax.fori_loop(0, pairs - 1, go_forward, 0)
    outward(out_f, in_f, f_send, f_recv, own - 1).wait_recv()
    forward(pairs - 1)
    homeward(out_o, in_o, o_send, o_recv, own - 1).start()
    in_o[own] = out_o[own]

    def backward(k):
        both = pl.ds(2 * k, 2)
        grads = in_g[both].reshape(2 * cap, channels)
        for at in range(0, hidden, tile):
            up = dot_t(grads, w2[at : at + tile, :])
            scale = slope[both, :, at : at + tile].reshape(2 * cap, tile)
            gate[both, :, at : at + tile] = (up * scale).astype(BF16).reshape(2, cap, tile)
        result = dot_t(gate[both].reshape(2 * cap, hidden), w1[...])
        out_b[both] = result.astype(BF16).reshape(2, cap, width)

    def got_grads(i):
        outward(out_g, in_g, g_send, g_recv, i).wait_recv()

    def send_back(i, carry):
        homeward(out_b, in_b, b_send, b_recv, i).start()
        return carry

    def go_backward(k, carry):
        got_grads(2 * k)
        got_grads(2 * k + 1)
        backward(k)
        return carry

    go_backward(0, 0)
    lax.fori_loop(0, 2, send_back, 0)
    lax.fori_loop(1, pairs - 1, go_backward, 0)
    got_grads(own - 1)
    backward(pairs - 1)
    in_b[own] = out_b[own]

    feats_t = in_f[...].reshape(slots, width).T
    grads_t = in_g[...].reshape(slots, channels).T
    pair = {}

    def weight_blocks(o):
        other = (level + o) % half
        for parity in range(2):
            start = pl.multiple_of((2 * other + parity) * block, block)
            part1[parity, other] = dot(
                feats_t, gate[:, :, pl.ds(start, block)].reshape(slots, block)).astype(BF16)
            part2[parity, other] = dot(
                grads_t, act[:, :, pl.ds(start, block)].reshape(slots, block)).astype(BF16)
        pair[o] = (
            remote(part1.at[1 - side, other], pair1.at[o],
                   pair_send.at[0, o], pair_recv.at[0, o], dp=mate),
            remote(part2.at[1 - side, other], pair2.at[o],
                   pair_send.at[1, o], pair_recv.at[1, o], dp=mate),
        )
        for copy in pair[o]:
            copy.start()

    def got_outs(i, carry):
        homeward(out_o, in_o, o_send, o_recv, i).wait_recv()
        return carry

    for o in list(range(1, half)) + [0]:
        weight_blocks(o)
    lax.fori_loop(0, own, got_outs, 0)
    back = spread[...].reshape(slots, tokens).T
    mixed = dot(back, in_o[...].reshape(slots, channels)).astype(BF16)
    grid_o[1 : rows + 1, 1] = mixed.reshape(rows, depth, channels)
    begin(halo_o)
    lax.fori_loop(2, own, send_back, 0)
    far = []
    for o in range(1, half):
        other = (level + o) % half
        for copy in pair[o]:
            copy.wait()
        sum1[o] = (part1[side, other].astype(F32) + pair1[o].astype(F32)).astype(BF16)
        sum2[o] = (part2[side, other].astype(F32) + pair2[o].astype(F32)).astype(BF16)
        to = 2 * other + side
        far.append(remote(
            sum1.at[o], far1.at[o], far_send.at[0, o], far_recv.at[0, o], dp=to))
        far.append(remote(
            sum2.at[o], far2.at[o], far_send.at[1, o], far_recv.at[1, o], dp=to))
        far[-2].start()
        far[-1].start()
    landed(halo_o)
    imitated[...] = convolved(grid_o, taps, rows, depth, False).astype(BF16)
    stores[0].start()
    finish(halo_o)
    for copy in pair[0]:
        copy.wait()
    for copy in far:
        copy.wait()
    total1 = part1[side, level].astype(F32) + pair1[0].astype(F32)
    total2 = part2[side, level].astype(F32) + pair2[0].astype(F32)
    for o in range(1, half):
        total1 = total1 + far1[o].astype(F32)
        total2 = total2 + far2[o].astype(F32)
    grad_one[...] = total1
    grad_two[...] = total2.T
    stores[1].start()
    stores[2].start()

    def got_back(i, carry):
        homeward(out_b, in_b, b_send, b_recv, i).wait_recv()
        return carry

    lax.fori_loop(0, pairs, got_back, 0)
    middle = pairs * cap
    early = dot(back[:, :middle], in_b[:pairs].reshape(middle, width))
    lax.fori_loop(pairs, own, got_back, 0)
    late = dot(back[:, middle:], in_b[pairs:].reshape(middle, width))
    feat_grad[...] = (early + late).astype(BF16)
    stores[3].start()

    def drained(i, carry):
        outward(out_f, in_f, f_send, f_recv, i).wait_send()
        outward(out_g, in_g, g_send, g_recv, i).wait_send()
        homeward(out_o, in_o, o_send, o_recv, i).wait_send()
        homeward(out_b, in_b, b_send, b_recv, i).wait_send()
        return carry

    lax.fori_loop(0, own, drained, 0)
    for copy in stores:
        copy.wait()


def handed_on(*refs):
    count = (len(refs) - 2) // 3
    news, olds, held = refs[count : 2 * count], refs[:count], refs[2 * count : 3 * count]
    in_sem, out_sem = refs[-2:]
    reads = [pltpu.make_async_copy(olds[i], held[i], in_sem.at[i]) for i in range(count)]
    writes = [pltpu.make_async_copy(held[i], news[i], out_sem.at[i]) for i in range(count)]
    for copy in reads:
        copy.start()
    for read, write in zip(reads, writes):
        read.wait()
        write.start()
    for copy in writes:
        copy.wait()


def per_device(feats, labels, w_first, w_second, taps, cotangent):
    n_dp = lax.axis_size("dp")
    n_ex = lax.axis_size("expert")
    rows, depth, width = feats.shape[1:]
    channels = taps.shape[2]
    hidden = w_first.shape[2]
    tokens = rows * depth
    cap = 2 * tokens // n_ex
    block = hidden // n_dp
    half = n_dp // 2
    hbm = pl.BlockSpec(memory_space=pltpu.HBM)
    wide = pltpu.VMEM((n_ex, cap, width), BF16)
    thin = pltpu.VMEM((n_ex, cap, channels), BF16)
    grid = pltpu.VMEM((rows + 2, 3, depth, channels), BF16)
    dma = pltpu.SemaphoreType.DMA
    outs = pl.pallas_call(
        functools.partial(kernel, n_dp, n_ex),
        out_shape=(
            jax.ShapeDtypeStruct((tokens, channels), BF16),
            jax.ShapeDtypeStruct((tokens, width), BF16),
            jax.ShapeDtypeStruct((width, block), F32),
            jax.ShapeDtypeStruct((block, channels), F32),
        ),
        in_specs=[hbm] * 6,
        out_specs=(hbm,) * 4,
        scratch_shapes=[
            pltpu.VMEM((tokens, channels), BF16),
            pltpu.VMEM((tokens, width), BF16),
            pltpu.VMEM((width, block), F32),
            pltpu.VMEM((block, channels), F32),
            pltpu.VMEM((1, tokens), jnp.int32),
            pltpu.VMEM((tokens, width), BF16),
            pltpu.VMEM((width, hidden), BF16),
            pltpu.VMEM((hidden, channels), BF16),
            pltpu.VMEM(taps.shape, BF16),
            pltpu.VMEM((n_ex, cap, tokens), BF16),
            wide, wide, thin, thin, thin, thin, wide, wide,
            pltpu.VMEM((n_ex, cap, hidden), BF16),
            pltpu.VMEM((n_ex, cap, hidden), F32),
            pltpu.VMEM((n_ex, cap, hidden), BF16),
            grid, grid,
            pltpu.VMEM((2, half, width, block), BF16),
            pltpu.VMEM((2, half, channels, block), BF16),
            pltpu.VMEM((half, width, block), BF16),
            pltpu.VMEM((half, channels, block), BF16),
            pltpu.VMEM((half, width, block), BF16),
            pltpu.VMEM((half, channels, block), BF16),
            pltpu.VMEM((half, width, block), BF16),
            pltpu.VMEM((half, channels, block), BF16),
            dma((6,)), dma((4,)), dma((12,)), dma((12,)),
            dma((n_ex,)), dma((n_ex,)), dma((n_ex,)), dma((n_ex,)),
            dma((n_ex,)), dma((n_ex,)), dma((n_ex,)), dma((n_ex,)),
            dma((2, half)), dma((2, half)), dma((2, half)), dma((2, half)),
        ],
        compiler_params=pltpu.CompilerParams(
            collective_id=0, has_side_effects=True, vmem_limit_bytes=60 * 2**20
        ),
        name="routed_experts",
    )(
        labels.reshape(1, tokens),
        feats.reshape(tokens, width),
        cotangent.reshape(rows, depth, channels),
        w_first[0],
        w_second[0],
        taps,
    )
    imitated, feat_grad, grad_one, grad_two = pl.pallas_call(
        handed_on,
        out_shape=tuple(jax.ShapeDtypeStruct(x.shape, x.dtype) for x in outs),
        in_specs=[hbm] * 4,
        out_specs=(hbm,) * 4,
        scratch_shapes=[pltpu.VMEM(x.shape, x.dtype) for x in outs] + [dma((4,)), dma((4,))],
        compiler_params=pltpu.CompilerParams(vmem_limit_bytes=60 * 2**20),
        name="handed_on",
    )(*outs)
    return (
        imitated.reshape(1, rows, depth, channels),
        feat_grad.reshape(1, rows, depth, width),
        grad_one[None],
        grad_two[None],
    )


def solution(mesh):
    in_specs = (
        P("dp", "expert", None, None),
        P("dp", "expert", None, None),
        P("expert", None, None),
        P("expert", None, None),
        P(),
        P("dp", "expert", None, None),
    )
    out_specs = (
        P("dp", "expert", None, None),
        P("dp", "expert", None, None),
        P("expert", None, "dp"),
        P("expert", "dp", None),
    )
    return jax.shard_map(
        per_device, mesh=mesh, in_specs=in_specs, out_specs=out_specs, check_vma=False
    )
```

```python
import functools

import jax
import jax.numpy as jnp
from jax import lax
from jax.experimental import pallas as pl
from jax.experimental.pallas import tpu as pltpu
from jax.sharding import PartitionSpec as P

BF16 = jnp.bfloat16
F32 = jnp.float32
ROOT = 0.7978845608028654
CUBIC = 0.044715


def dot(a, b):
    return jnp.dot(a, b, preferred_element_type=F32)


def dot_t(a, b):
    return lax.dot_general(a, b, (((1,), (1,)), ((), ())), preferred_element_type=F32)


def remote(src, dst, send, recv, **device):
    return pltpu.make_async_remote_copy(
        src_ref=src,
        dst_ref=dst,
        send_sem=send,
        recv_sem=recv,
        device_id=device,
        device_id_type=pl.DeviceIdType.MESH,
    )


def shifted(value, step, depth):
    rows = value.shape[0]
    place = lax.broadcasted_iota(jnp.int32, value.shape, 0) % depth
    if step > 0:
        return jnp.where(place == 0, 0.0, pltpu.roll(value, 1, 0))
    return jnp.where(place == depth - 1, 0.0, pltpu.roll(value, rows - 1, 0))


def convolved(grid, taps, rows, depth, flipped):
    channels = taps.shape[1]
    tokens = rows * depth
    pieces, sums = [], []
    for a in range(3):
        for b in range(3):
            at, bt = (2 - a, 2 - b) if flipped else (a, b)
            pieces.append(grid[bt : bt + rows, at].reshape(tokens, channels))
    columns = jnp.concatenate(pieces, axis=1)
    for c in range(3):
        if flipped:
            weights = jnp.concatenate([taps[3 * k + c] for k in range(9)], axis=1)
            sums.append(dot_t(columns, weights))
        else:
            weights = jnp.concatenate([taps[3 * k + c] for k in range(9)], axis=0)
            sums.append(dot(columns, weights))
    first, last = (sums[2], sums[0]) if flipped else (sums[0], sums[2])
    return sums[1] + shifted(first, 1, depth) + shifted(last, -1, depth)


def kernel(
    n_dp, n_ex,
    labels_hbm, feats_hbm, cot_hbm, w1_hbm, w2_hbm, taps_hbm,
    imitated_hbm, feat_grad_hbm, grad_one_hbm, grad_two_hbm,
    imitated, feat_grad, grad_one, grad_two,
    labels, feats, w1, w2, taps, spread,
    out_f, in_f, out_g, in_g, out_o, in_o, out_b, in_b,
    act, slope, gate, grid_g, grid_o,
    part1, part2, pair1, pair2, sum1, sum2, far1, far2,
    load_sem, store_sem, halo_send, halo_recv,
    f_send, f_recv, g_send, g_recv, o_send, o_recv, b_send, b_recv,
    pair_send, pair_recv, far_send, far_recv,
):
    tokens, width = feats.shape
    rows, depth, channels = cot_hbm.shape
    hidden = w1.shape[1]
    cap = in_f.shape[1]
    slots = n_ex * cap
    block = hidden // n_dp
    half = n_dp // 2
    dp = lax.axis_index("dp")
    me = lax.axis_index("expert")
    side = dp % 2
    level = dp // 2
    mate = dp + 1 - 2 * side

    loads = [
        pltpu.make_async_copy(w1_hbm, w1, load_sem.at[0]),
        pltpu.make_async_copy(w2_hbm, w2, load_sem.at[1]),
        pltpu.make_async_copy(taps_hbm, taps, load_sem.at[2]),
        pltpu.make_async_copy(labels_hbm, labels, load_sem.at[3]),
        pltpu.make_async_copy(cot_hbm, grid_g.at[pl.ds(1, rows), 1], load_sem.at[4]),
        pltpu.make_async_copy(feats_hbm, feats, load_sem.at[5]),
    ]
    for at in (3, 4, 5, 2, 0, 1):
        loads[at].start()

    stores = [
        pltpu.make_async_copy(imitated, imitated_hbm, store_sem.at[0]),
        pltpu.make_async_copy(grad_one, grad_one_hbm, store_sem.at[1]),
        pltpu.make_async_copy(grad_two, grad_two_hbm, store_sem.at[2]),
        pltpu.make_async_copy(feat_grad, feat_grad_hbm, store_sem.at[3]),
    ]

    barrier = pltpu.get_barrier_semaphore()

    def greet_expert(d, carry):
        pl.semaphore_signal(
            barrier, inc=1, device_id={"expert": (me + d) % n_ex},
            device_id_type=pl.DeviceIdType.MESH,
        )
        return carry

    def greet_dp(d, carry):
        pl.semaphore_signal(
            barrier, inc=1, device_id={"dp": (dp + d) % n_dp},
            device_id_type=pl.DeviceIdType.MESH,
        )
        return carry

    for x in (1, n_dp - 1):
        for y in (1, n_ex - 1):
            pl.semaphore_signal(
                barrier, inc=1,
                device_id={"dp": (dp + x) % n_dp, "expert": (me + y) % n_ex},
                device_id_type=pl.DeviceIdType.MESH,
            )
    lax.fori_loop(1, n_ex, greet_expert, 0)
    lax.fori_loop(1, n_dp, greet_dp, 0)
    loads[3].wait()

    relative = labels[...] - me
    relative = jnp.where(relative < 0, relative + n_ex, relative)
    relative = jnp.where(
        relative >= n_ex // 2, 2 * relative - n_ex, n_ex - 1 - 2 * relative)
    named = lax.broadcasted_iota(jnp.int32, (n_ex, tokens), 0)
    hot = relative == named
    before = (
        lax.broadcasted_iota(jnp.int32, (tokens, tokens), 0)
        < lax.broadcasted_iota(jnp.int32, (tokens, tokens), 1)
    )
    rank = dot(jnp.where(hot, 1.0, 0.0).astype(BF16), jnp.where(before, 1.0, 0.0).astype(BF16))
    place = rank + (named * cap).astype(F32)
    target = jnp.sum(jnp.where(hot, place, 0.0), axis=0, keepdims=True)
    which = lax.broadcasted_iota(jnp.int32, (cap, tokens), 0)

    def halo(grid, at):
        return (
            (me < n_ex - 1, me > 0, remote(
                grid.at[rows, 1], grid.at[0, 1],
                halo_send.at[at], halo_recv.at[at], expert=(me + 1) % n_ex)),
            (me > 0, me < n_ex - 1, remote(
                grid.at[1, 1], grid.at[rows + 1, 1],
                halo_send.at[at + 1], halo_recv.at[at + 1], expert=(me + n_ex - 1) % n_ex)),
            (dp < n_dp - 1, dp > 0, remote(
                grid.at[:, 1], grid.at[:, 0],
                halo_send.at[at + 2], halo_recv.at[at + 2], dp=(dp + 1) % n_dp)),
            (dp > 0, dp < n_dp - 1, remote(
                grid.at[:, 1], grid.at[:, 2],
                halo_send.at[at + 3], halo_recv.at[at + 3], dp=(dp + n_dp - 1) % n_dp)),
        )

    def begin(steps):
        for sends, _, copy in steps:
            pl.when(sends)(copy.start)

    def landed(steps):
        for _, gets, copy in steps:
            pl.when(gets)(copy.wait_recv)

    def finish(steps):
        for sends, _, copy in steps:
            pl.when(sends)(copy.wait_send)

    def edges(grid):
        slab = jnp.zeros((rows + 2, depth, channels), BF16)
        strip = jnp.zeros((depth, channels), BF16)

        @pl.when(dp == 0)
        def _():
            grid[:, 0] = slab

        @pl.when(dp == n_dp - 1)
        def _():
            grid[:, 2] = slab

        @pl.when(me == 0)
        def _():
            grid[0, 1] = strip

        @pl.when(me == n_ex - 1)
        def _():
            grid[rows + 1, 1] = strip

    def halo_at_once(grid, at):
        inner = pl.ds(1, rows)
        steps = []
        for x in (-1, 0, 1):
            for y in (-1, 0, 1):
                if x == 0 and y == 0:
                    continue
                mine = {-1: 1, 0: inner, 1: rows}[y]
                theirs = {-1: rows + 1, 0: inner, 1: 0}[y]
                near = True
                come = True
                if x != 0:
                    near = dp < n_dp - 1 if x > 0 else dp > 0
                    come = dp > 0 if x > 0 else dp < n_dp - 1
                if y != 0:
                    goes = me < n_ex - 1 if y > 0 else me > 0
                    gets = me > 0 if y > 0 else me < n_ex - 1
                    near = goes if x == 0 else jnp.logical_and(near, goes)
                    come = gets if x == 0 else jnp.logical_and(come, gets)
                spot = at + len(steps)
                steps.append((near, come, remote(
                    grid.at[mine, 1], grid.at[theirs, 1 - x],
                    halo_send.at[spot], halo_recv.at[spot],
                    dp=(dp + x + n_dp) % n_dp, expert=(me + y + n_ex) % n_ex)))
        return steps

    halo_g, halo_o = halo(grid_g, 0), halo_at_once(grid_o, 4)
    loads[4].wait()
    pl.semaphore_wait(barrier, n_ex + n_dp + 2)
    begin(halo_g[:2])
    loads[5].wait()

    def turn(i):
        return n_ex // 2 + (1 - 2 * (i % 2)) * ((i + 1) // 2)

    def outward(src, dst, send, recv, i):
        return remote(
            src.at[i], dst.at[i], send.at[i], recv.at[i], expert=(me + turn(i)) % n_ex
        )

    def homeward(src, dst, send, recv, i):
        return remote(
            src.at[i], dst.at[i], send.at[i], recv.at[i], expert=(me + n_ex - turn(i)) % n_ex
        )

    def chosen(i):
        hit = (which + i * cap).astype(F32) == target
        return jnp.where(hit, 1.0, 0.0).astype(BF16)

    def send_feats(i, carry):
        spread[i] = chosen(i)
        out_f[i] = dot(spread[i], feats[...]).astype(BF16)
        outward(out_f, in_f, f_send, f_recv, i).start()
        return carry

    own = n_ex - 1
    lax.fori_loop(0, 2, send_feats, 0)
    edges(grid_g)
    edges(grid_o)
    strips = jnp.zeros((3, depth, channels), BF16)

    @pl.when(me == 0)
    def _():
        grid_o[0] = strips

    @pl.when(me == n_ex - 1)
    def _():
        grid_o[rows + 1] = strips

    landed(halo_g[:2])
    begin(halo_g[2:])
    lax.fori_loop(2, own, send_feats, 0)
    spread[own] = chosen(own)
    in_f[own] = dot(spread[own], feats[...]).astype(BF16)

    tile = min(hidden, 512)
    loads[2].wait()
    landed(halo_g[2:])
    field_grad = convolved(grid_g, taps, rows, depth, True).astype(BF16)
    grid_o[1 : rows + 1, 1] = field_grad.reshape(rows, depth, channels)

    def send_grads(i, carry):
        out_g[i] = dot(spread[i], grid_o[1 : rows + 1, 1].reshape(tokens, channels)).astype(BF16)
        outward(out_g, in_g, g_send, g_recv, i).start()
        return carry

    lax.fori_loop(0, own, send_grads, 0)
    in_g[own] = dot(spread[own], grid_o[1 : rows + 1, 1].reshape(tokens, channels)).astype(BF16)
    finish(halo_g)
    loads[0].wait()
    loads[1].wait()

    def forward(k):
        both = pl.ds(2 * k, 2)
        row_block = in_f[both].reshape(2 * cap, width)
        for at in range(0, hidden, tile):
            v = dot(row_block, w1[:, at : at + tile])
            square = v * v
            t = jnp.tanh(v * (ROOT + (ROOT * CUBIC) * square))
            half_up = 0.5 + 0.5 * t
            act[both, :, at : at + tile] = (v * half_up).astype(BF16).reshape(2, cap, tile)
            inner = ROOT + (3.0 * ROOT * CUBIC) * square
            grown = half_up + (0.5 * v) * (1.0 - t * t) * inner
            slope[both, :, at : at + tile] = grown.reshape(2, cap, tile)
        result = dot(act[both].reshape(2 * cap, hidden), w2[...])
        out_o[both] = result.astype(BF16).reshape(2, cap, channels)

    def go_forward(k, carry):
        for i in (2 * k, 2 * k + 1):
            outward(out_f, in_f, f_send, f_recv, i).wait_recv()
        forward(k)
        for i in (2 * k, 2 * k + 1):
            homeward(out_o, in_o, o_send, o_recv, i).start()
        return carry

    pairs = n_ex // 2
    lax.fori_loop(0, pairs - 1, go_forward, 0)
    outward(out_f, in_f, f_send, f_recv, own - 1).wait_recv()
    forward(pairs - 1)
    homeward(out_o, in_o, o_send, o_recv, own - 1).start()
    in_o[own] = out_o[own]

    def backward(k):
        both = pl.ds(2 * k, 2)
        grads = in_g[both].reshape(2 * cap, channels)
        for at in range(0, hidden, tile):
            up = dot_t(grads, w2[at : at + tile, :])
            scale = slope[both, :, at : at + tile].reshape(2 * cap, tile)
            gate[both, :, at : at + tile] = (up * scale).astype(BF16).reshape(2, cap, tile)
        result = dot_t(gate[both].reshape(2 * cap, hidden), w1[...])
        out_b[both] = result.astype(BF16).reshape(2, cap, width)

    def got_grads(i):
        outward(out_g, in_g, g_send, g_recv, i).wait_recv()

    def send_back(i, carry):
        homeward(out_b, in_b, b_send, b_recv, i).start()
        return carry

    def go_backward(k, carry):
        got_grads(2 * k)
        got_grads(2 * k + 1)
        backward(k)
        return carry

    go_backward(0, 0)
    lax.fori_loop(0, 2, send_back, 0)
    lax.fori_loop(1, pairs - 1, go_backward, 0)
    got_grads(own - 1)
    backward(pairs - 1)
    in_b[own] = out_b[own]

    feats_t = in_f[...].reshape(slots, width).T
    grads_t = in_g[...].reshape(slots, channels).T
    pair = {}

    def weight_blocks(o):
        other = (level + o) % half
        for parity in range(2):
            start = pl.multiple_of((2 * other + parity) * block, block)
            part1[parity, other] = dot(
                feats_t, gate[:, :, pl.ds(start, block)].reshape(slots, block)).astype(BF16)
            part2[parity, other] = dot(
                grads_t, act[:, :, pl.ds(start, block)].reshape(slots, block)).astype(BF16)
        pair[o] = (
            remote(part1.at[1 - side, other], pair1.at[o],
                   pair_send.at[0, o], pair_recv.at[0, o], dp=mate),
            remote(part2.at[1 - side, other], pair2.at[o],
                   pair_send.at[1, o], pair_recv.at[1, o], dp=mate),
        )
        for copy in pair[o]:
            copy.start()

    def got_outs(i, carry):
        homeward(out_o, in_o, o_send, o_recv, i).wait_recv()
        return carry

    for o in range(1, half):
        weight_blocks(o)
    lax.fori_loop(0, own, got_outs, 0)
    back = spread[...].reshape(slots, tokens).T
    mixed = dot(back, in_o[...].reshape(slots, channels)).astype(BF16)
    grid_o[1 : rows + 1, 1] = mixed.reshape(rows, depth, channels)
    begin(halo_o)
    lax.fori_loop(2, own, send_back, 0)
    far = []
    for o in range(1, half):
        other = (level + o) % half
        for copy in pair[o]:
            copy.wait()
        sum1[o] = (part1[side, other].astype(F32) + pair1[o].astype(F32)).astype(BF16)
        sum2[o] = (part2[side, other].astype(F32) + pair2[o].astype(F32)).astype(BF16)
        to = 2 * other + side
        far.append(remote(
            sum1.at[o], far1.at[o], far_send.at[0, o], far_recv.at[0, o], dp=to))
        far.append(remote(
            sum2.at[o], far2.at[o], far_send.at[1, o], far_recv.at[1, o], dp=to))
        far[-2].start()
        far[-1].start()
    weight_blocks(0)
    landed(halo_o)
    imitated[...] = convolved(grid_o, taps, rows, depth, False).astype(BF16)
    stores[0].start()
    finish(halo_o)
    for copy in pair[0]:
        copy.wait()
    for copy in far:
        copy.wait()
    total1 = part1[side, level].astype(F32) + pair1[0].astype(F32)
    total2 = part2[side, level].astype(F32) + pair2[0].astype(F32)
    for o in range(1, half):
        total1 = total1 + far1[o].astype(F32)
        total2 = total2 + far2[o].astype(F32)
    grad_one[...] = total1
    grad_two[...] = total2.T
    stores[1].start()
    stores[2].start()

    def got_back(i, carry):
        homeward(out_b, in_b, b_send, b_recv, i).wait_recv()
        return carry

    lax.fori_loop(0, pairs, got_back, 0)
    middle = pairs * cap
    early = dot(back[:, :middle], in_b[:pairs].reshape(middle, width))
    lax.fori_loop(pairs, own, got_back, 0)
    late = dot(back[:, middle:], in_b[pairs:].reshape(middle, width))
    feat_grad[...] = (early + late).astype(BF16)
    stores[3].start()

    def drained(i, carry):
        outward(out_f, in_f, f_send, f_recv, i).wait_send()
        outward(out_g, in_g, g_send, g_recv, i).wait_send()
        homeward(out_o, in_o, o_send, o_recv, i).wait_send()
        homeward(out_b, in_b, b_send, b_recv, i).wait_send()
        return carry

    lax.fori_loop(0, own, drained, 0)
    for copy in stores:
        copy.wait()


def handed_on(*refs):
    count = (len(refs) - 2) // 3
    news, olds, held = refs[count : 2 * count], refs[:count], refs[2 * count : 3 * count]
    in_sem, out_sem = refs[-2:]
    reads = [pltpu.make_async_copy(olds[i], held[i], in_sem.at[i]) for i in range(count)]
    writes = [pltpu.make_async_copy(held[i], news[i], out_sem.at[i]) for i in range(count)]
    for copy in reads:
        copy.start()
    for read, write in zip(reads, writes):
        read.wait()
        write.start()
    for copy in writes:
        copy.wait()


def per_device(feats, labels, w_first, w_second, taps, cotangent):
    n_dp = lax.axis_size("dp")
    n_ex = lax.axis_size("expert")
    rows, depth, width = feats.shape[1:]
    channels = taps.shape[2]
    hidden = w_first.shape[2]
    tokens = rows * depth
    cap = 2 * tokens // n_ex
    block = hidden // n_dp
    half = n_dp // 2
    hbm = pl.BlockSpec(memory_space=pltpu.HBM)
    wide = pltpu.VMEM((n_ex, cap, width), BF16)
    thin = pltpu.VMEM((n_ex, cap, channels), BF16)
    grid = pltpu.VMEM((rows + 2, 3, depth, channels), BF16)
    dma = pltpu.SemaphoreType.DMA
    outs = pl.pallas_call(
        functools.partial(kernel, n_dp, n_ex),
        out_shape=(
            jax.ShapeDtypeStruct((tokens, channels), BF16),
            jax.ShapeDtypeStruct((tokens, width), BF16),
            jax.ShapeDtypeStruct((width, block), F32),
            jax.ShapeDtypeStruct((block, channels), F32),
        ),
        in_specs=[hbm] * 6,
        out_specs=(hbm,) * 4,
        scratch_shapes=[
            pltpu.VMEM((tokens, channels), BF16),
            pltpu.VMEM((tokens, width), BF16),
            pltpu.VMEM((width, block), F32),
            pltpu.VMEM((block, channels), F32),
            pltpu.VMEM((1, tokens), jnp.int32),
            pltpu.VMEM((tokens, width), BF16),
            pltpu.VMEM((width, hidden), BF16),
            pltpu.VMEM((hidden, channels), BF16),
            pltpu.VMEM(taps.shape, BF16),
            pltpu.VMEM((n_ex, cap, tokens), BF16),
            wide, wide, thin, thin, thin, thin, wide, wide,
            pltpu.VMEM((n_ex, cap, hidden), BF16),
            pltpu.VMEM((n_ex, cap, hidden), F32),
            pltpu.VMEM((n_ex, cap, hidden), BF16),
            grid, grid,
            pltpu.VMEM((2, half, width, block), BF16),
            pltpu.VMEM((2, half, channels, block), BF16),
            pltpu.VMEM((half, width, block), BF16),
            pltpu.VMEM((half, channels, block), BF16),
            pltpu.VMEM((half, width, block), BF16),
            pltpu.VMEM((half, channels, block), BF16),
            pltpu.VMEM((half, width, block), BF16),
            pltpu.VMEM((half, channels, block), BF16),
            dma((6,)), dma((4,)), dma((12,)), dma((12,)),
            dma((n_ex,)), dma((n_ex,)), dma((n_ex,)), dma((n_ex,)),
            dma((n_ex,)), dma((n_ex,)), dma((n_ex,)), dma((n_ex,)),
            dma((2, half)), dma((2, half)), dma((2, half)), dma((2, half)),
        ],
        compiler_params=pltpu.CompilerParams(
            collective_id=0, has_side_effects=True, vmem_limit_bytes=60 * 2**20
        ),
        name="routed_experts",
    )(
        labels.reshape(1, tokens),
        feats.reshape(tokens, width),
        cotangent.reshape(rows, depth, channels),
        w_first[0],
        w_second[0],
        taps,
    )
    imitated, feat_grad, grad_one, grad_two = pl.pallas_call(
        handed_on,
        out_shape=tuple(jax.ShapeDtypeStruct(x.shape, x.dtype) for x in outs),
        in_specs=[hbm] * 4,
        out_specs=(hbm,) * 4,
        scratch_shapes=[pltpu.VMEM(x.shape, x.dtype) for x in outs] + [dma((4,)), dma((4,))],
        compiler_params=pltpu.CompilerParams(vmem_limit_bytes=60 * 2**20),
        name="handed_on",
    )(*outs)
    return (
        imitated.reshape(1, rows, depth, channels),
        feat_grad.reshape(1, rows, depth, width),
        grad_one[None],
        grad_two[None],
    )


def solution(mesh):
    in_specs = (
        P("dp", "expert", None, None),
        P("dp", "expert", None, None),
        P("expert", None, None),
        P("expert", None, None),
        P(),
        P("dp", "expert", None, None),
    )
    out_specs = (
        P("dp", "expert", None, None),
        P("dp", "expert", None, None),
        P("expert", None, "dp"),
        P("expert", "dp", None),
    )
    return jax.shard_map(
        per_device, mesh=mesh, in_specs=in_specs, out_specs=out_specs, check_vma=False
    )
```
